32 devices in a mesh: batch: 4 (over z), proto: 8 (over y, x, core).
Axes of the slice: x: 2, y: 2, z: 4, core: 2. Of those that a mesh axis runs over, the one named last changes fastest.
Arguments:
- teacher_feats: bfloat16 [1024, 256], P('batch'), may hold values from -2 to 2
- student_feats: bfloat16 [1024, 256], P('batch'), may hold values from -2 to 2
- teacher_weight: bfloat16 [256, 32768], P(None, 'proto'), may hold values from -2 to 2
- student_weight: bfloat16 [256, 32768], P(None, 'proto'), may hold values from -2 to 2
Outputs:
- weight_grad: bfloat16 [256, 32768], P('batch', 'proto')
- feature_grad: bfloat16 [1024, 256], P('batch')
The draws below stay inside these ranges and needn't reach their ends.
All inputs are finite; a program needn't handle non-finite values.
Results may differ from the reference program's by a relative error of at most 0.025.
Values may be sent and summed in bfloat16 or wider, within the bound.
No kernel may reach another device: no remote copies, remote signals or barrier semaphores. Data moves between devices by JAX's collectives and lax.ppermute only.
A program may use at most 64 MiB of HBM per device.

```python
import math
import jax
import jax.numpy as jnp
from jax import lax

D = 256
B_DEV = 256
ITERS = 3
CLUSTERS = 64
PROTOS = 32768
CROPS = 1024


def cluster_parts(key):
    centres = jax.random.normal(jax.random.fold_in(key, 101), (CLUSTERS, D), jnp.float32)
    crop_ids = jnp.sort(jax.random.randint(jax.random.fold_in(key, 102), (CROPS,), 0, CLUSTERS))
    first_ids = jax.random.randint(jax.random.fold_in(key, 103), (PROTOS,), 0, CLUSTERS)
    second_ids = jax.random.randint(jax.random.fold_in(key, 104), (PROTOS,), 0, CLUSTERS)
    proto_ids = jnp.sort(jnp.minimum(first_ids, second_ids))
    crop_shared = jax.random.normal(jax.random.fold_in(key, 105), (CROPS, D), jnp.float32)
    proto_shared = jax.random.normal(jax.random.fold_in(key, 106), (D, PROTOS), jnp.float32)
    return (centres, crop_ids, proto_ids, crop_shared, proto_shared)


def draw_teacher_feats(key, part):
    centres, crop_ids, proto_ids, crop_shared, proto_shared = cluster_parts(key)
    key = jax.random.fold_in(key, 1)
    strength = 0.65
    noise = jax.random.normal(key, (CROPS, D), jnp.float32)
    values = (strength * centres[crop_ids] + 0.7 * crop_shared + 0.7 * noise) / 16.0
    return jnp.clip(values, -2.0, 2.0).astype(jnp.bfloat16)


def draw_student_feats(key, part):
    centres, crop_ids, proto_ids, crop_shared, proto_shared = cluster_parts(key)
    key = jax.random.fold_in(key, 2)
    strength = 0.65
    noise = jax.random.normal(key, (CROPS, D), jnp.float32)
    values = (strength * centres[crop_ids] + 0.7 * crop_shared + 0.7 * noise) / 16.0
    return jnp.clip(values, -2.0, 2.0).astype(jnp.bfloat16)


def draw_teacher_weight(key, part):
    centres, crop_ids, proto_ids, crop_shared, proto_shared = cluster_parts(key)
    key = jax.random.fold_in(key, 3)
    strength = 0.65
    noise = jax.random.normal(key, (D, PROTOS), jnp.float32)
    values = (strength * centres[proto_ids].T + 0.7 * proto_shared + 0.7 * noise) / 16.0
    return jnp.clip(values, -2.0, 2.0).astype(jnp.bfloat16)


def draw_student_weight(key, part):
    centres, crop_ids, proto_ids, crop_shared, proto_shared = cluster_parts(key)
    key = jax.random.fold_in(key, 4)
    strength = 0.65
    noise = jax.random.normal(key, (D, PROTOS), jnp.float32)
    values = (strength * centres[proto_ids].T + 0.7 * proto_shared + 0.7 * noise) / 16.0
    return jnp.clip(values, -2.0, 2.0).astype(jnp.bfloat16)


def setup_inputs(seed: int = 0) -> dict:
    seeds = jax.random.split(jax.random.key(seed), 5)
    teacher_feats = draw_teacher_feats(jax.random.fold_in(seeds[4], 71), 0)
    student_feats = draw_student_feats(jax.random.fold_in(seeds[4], 71), 0)
    teacher_weight = draw_teacher_weight(jax.random.fold_in(seeds[4], 71), 0)
    student_weight = draw_student_weight(jax.random.fold_in(seeds[4], 71), 0)
    return dict(teacher_feats=teacher_feats, student_feats=student_feats, teacher_weight=teacher_weight, student_weight=student_weight)


teacher_temp = 0.07
student_temp = 0.1
epsilon = 1e-06

def unit_rows(raw):
    values = raw.astype(jnp.float32)
    length = jnp.sqrt(lax.optimization_barrier(jnp.sum(values * values, axis=1, keepdims=True)) + epsilon)
    return (values / length, length)

def unit_columns(raw):
    values = raw.astype(jnp.float32)
    length = jnp.sqrt(lax.optimization_barrier(jnp.sum(values * values, axis=0, keepdims=True)) + epsilon)
    return (values / length).astype(jnp.bfloat16)

def reference(teacher_feats, student_feats, teacher_weight, student_weight):
    teacher_unit, _ = unit_rows(teacher_feats)
    teacher_half = teacher_unit.astype(jnp.bfloat16)
    student_unit, student_len = unit_rows(student_feats)
    student_half = student_unit.astype(jnp.bfloat16)
    teacher_cols = unit_columns(teacher_weight)
    student_cols = unit_columns(student_weight)
    groups = CROPS // B_DEV
    teacher_blocks = teacher_half.reshape(groups, B_DEV, D)

    def teacher_exp(block):
        return jnp.exp(jnp.dot(block, teacher_cols, preferred_element_type=jnp.float32) / teacher_temp)
    crop_scale = jnp.ones((groups, B_DEV), jnp.float32)
    proto_scale = jnp.ones((PROTOS,), jnp.float32)
    for sweep_index in range(ITERS):

        def add_rows(total, item):
            block, scale = item
            return (total + lax.optimization_barrier(jnp.sum(teacher_exp(block) * scale[:, None], axis=0)), None)
        sums, _ = lax.scan(add_rows, jnp.zeros((PROTOS,), jnp.float32), (teacher_blocks, crop_scale))
        proto_scale = 1.0 / sums

        def crop_total(block):
            return lax.optimization_barrier(jnp.sum(teacher_exp(block) * proto_scale[None, :], axis=1))
        crop_scale = 1.0 / lax.map(crop_total, teacher_blocks)
    weight_factor = math.sqrt(D / CROPS)
    feature_factor = math.sqrt(D / PROTOS)

    def finish(carry, item):
        tblock, sblock, sfull, slength, scale = item
        targets = teacher_exp(tblock) * proto_scale[None, :] * scale[:, None]
        logits = jnp.dot(sblock, student_cols, preferred_element_type=jnp.float32) / student_temp
        log_total = jnp.log(lax.optimization_barrier(jnp.sum(jnp.exp(logits), axis=1, keepdims=True)))
        student_prob = jnp.exp(logits - log_total)
        grad_logits = (PROTOS * (student_prob - targets)).astype(jnp.bfloat16)
        partial_value = lax.dot_general(sblock, grad_logits, (((0,), (0,)), ((), ())), preferred_element_type=jnp.float32) * weight_factor
        partial_value = lax.optimization_barrier(partial_value.astype(jnp.bfloat16)).astype(jnp.float32)
        unit_grad = lax.dot_general(grad_logits, student_cols, (((1,), (1,)), ((), ())), preferred_element_type=jnp.float32) * feature_factor
        along = lax.optimization_barrier(jnp.sum(sfull * unit_grad, axis=1, keepdims=True))
        rows_grad = ((unit_grad - sfull * along) / slength).astype(jnp.bfloat16)
        return (carry + partial_value, rows_grad)
    start = jnp.zeros((D, PROTOS), jnp.float32)
    items = (teacher_blocks, student_half.reshape(groups, B_DEV, D), student_unit.reshape(groups, B_DEV, D), student_len.reshape(groups, B_DEV, 1), crop_scale)
    weight_total, rows_all = lax.scan(finish, start, items)
    return (weight_total.astype(jnp.bfloat16), rows_all.reshape(CROPS, D))
```

```python
import functools
import math

import jax
import jax.numpy as jnp
from jax import lax
from jax.experimental import pallas as pl
from jax.experimental.pallas import tpu as pltpu
from jax.sharding import PartitionSpec as P

ITERS = 3

teacher_temp = 0.07
student_temp = 0.1
epsilon = 1e-06
LOG2E = 1.4426950408889634
BF = jnp.bfloat16
F32 = jnp.float32
MIB = 1024 * 1024
BLK = 512
LANES = 128


def dot(a, b):
    return jnp.dot(a, b, preferred_element_type=F32)


def split(values):
    high = values.astype(BF).astype(F32)
    return high, (values - high).astype(BF).astype(F32)


def split_rows(row):
    high, low = split(row)
    at = lax.broadcasted_iota(jnp.int32, (16, row.shape[1]), 0)
    return jnp.where(at == 0, high, jnp.where(at == 1, low, 0.0)).astype(BF)


def unit_rows(raw):
    values = raw.astype(F32)
    length = jnp.sqrt(jnp.sum(values * values, axis=1, keepdims=True) + epsilon)
    return values / length, length


def over(count, size, body, carry):
    if count <= 4:
        for i in range(count):
            carry = body(pl.ds(i * size, size), carry)
        return carry

    def step(i, carry):
        return body(pl.ds(pl.multiple_of(i * size, size), size), carry)

    return lax.fori_loop(0, count, step, carry)


def chunks(span):
    for at in range(0, span.size, 64):
        start = span.start + at
        yield pl.ds(start if isinstance(start, int) else pl.multiple_of(start, 64), 64)


def block(i):
    return pl.ds(pl.multiple_of(i * BLK, BLK), BLK)


def each_step(low, high, body):
    for i in range(low, high):
        body(i)


def two_steps(steps, first, second):
    carry = first(0)
    for i in range(1, steps):
        second(i - 1, carry)
        carry = first(i)
    second(steps - 1, carry)


def lane_groups(values):
    out = values[:, :LANES]
    for at in range(LANES, values.shape[1], LANES):
        out = out + values[:, at : at + LANES]
    return out


def sublane_groups(values):
    return jnp.sum(values.reshape(-1, 8, values.shape[1]), axis=0)


def joined(total, nb, at=0):
    return total[at : at + nb] + total[at + nb : at + 2 * nb]


def blocks_of(crops):
    height = next(h for h in (768, 512, 256, crops) if crops % h == 0)
    return crops // height, height


def row_sums(nb, rows, acc, at=0):
    spans = [slice(at + i * rows, at + (i + 1) * rows) for i in range(nb)]
    return [jnp.sum(acc[span, :].T, axis=0, keepdims=True) for span in spans]


def put_sums(sums, out, at=0):
    for i, row in enumerate(sums):
        high, low = split(row)
        out[at + i : at + i + 1, :] = high
        out[at + len(sums) + i : at + len(sums) + i + 1, :] = low


def deal(hops, head, read, count, outs, kept, chips=0):
    many = 1 + len(hops)
    me = lax.axis_index("proto")
    digit = (me // hops[0]) % many
    for hop, out in zip((0, *hops), (kept, *outs)):
        out[0 : head.shape[0], :] = head[...].astype(out.dtype)
        for m in range(count // many):
            turn = (me // 2 % chips == m % chips).astype(jnp.int32) if chips else 0
            rows = read(m * many + (digit ^ (hop // hops[0]) ^ turn)).astype(out.dtype)
            at = head.shape[0] + m * rows.shape[0]
            out[at : at + rows.shape[0], :] = rows


def added(refs):
    acc = refs[0][...].astype(F32)
    for ref in refs[1:]:
        acc = acc + ref[...].astype(F32)
    return acc


def halves_kernel(teacher_ref, student_ref, out, sems):
    half = out.shape[0] * 2 // 3
    me = lax.axis_index("proto")
    start = pl.multiple_of(me % 2 * half, half)
    quarter = pl.multiple_of(start + me // 2 % 2 * (half // 2), half // 2)
    first = pltpu.make_async_copy(
        teacher_ref.at[pl.ds(start, half), :], out.at[0:half, :], sems.at[0]
    )
    second = pltpu.make_async_copy(
        student_ref.at[pl.ds(quarter, half // 2), :], out.at[half:, :], sems.at[1]
    )
    first.start()
    second.start()
    first.wait()
    second.wait()


def units_kernel(after, also, *refs):
    blocks, outs = refs[-3::-1], refs[-2:]
    start = 0
    for out in outs:
        size = out.shape[0] // len(blocks)
        for i, ref in enumerate(blocks):
            rows = unit_rows(ref[start : start + size, :])[0]
            out[i * size : (i + 1) * size, :] = rows.astype(BF)
        start += size


def quarters_kernel(size, after, mine, moved, out):
    side = lax.axis_index("proto") // 2 % 2
    for i in range(mine.shape[0] // size):
        for ref, place in ((mine, side), (moved, 1 - side)):
            at = pl.multiple_of((2 * i + place) * size, size)
            out[pl.ds(at, size), :] = ref[i * size : (i + 1) * size, :]


def place_kernel(mine, other, out):
    far = mine.shape[0]
    core = lax.axis_index("proto") % 2
    for ref, place in ((mine, core), (other, 1 - core)):
        out[pl.ds(pl.multiple_of(place * far, 128), far), :] = ref[...]


def weights_kernel(wt_ref, ws_ref, wt_out, ws_out, turned_out, raw, sems):
    steps = wt_out.shape[0]

    def copy(i, which):
        src = (wt_ref, ws_ref)[which]
        return pltpu.make_async_copy(src.at[:, block(i)], raw.at[which, i], sems.at[which, i])

    for which in range(2):
        for i in range(steps):
            copy(i, which).start()

    def unit(i, which):
        copy(i, which).wait()
        values = raw[which, i].astype(F32)
        length = jnp.sqrt(jnp.sum(values * values, axis=0, keepdims=True) + epsilon)
        return (values * ((LOG2E / (teacher_temp, student_temp)[which]) / length)).astype(BF)

    def teacher(i):
        wt_out[i] = unit(i, 0)

    def student(i):
        ws = unit(i, 1)
        ws_out[i] = ws
        turned_out[i] = ws.T

    each_step(0, steps, teacher)
    each_step(0, steps, student)


def add_across(rows, refs, i, ps, acc):
    own, rest = refs
    ps = ps.astype(BF)

    def across(ref, start):
        def step(span, carry):
            for at in chunks(span):
                to = pl.ds(at.start + start, at.size)
                scaled = ref[i, at, :] * ps
                half = scaled[:, : BLK // 2] + scaled[:, BLK // 2 :]
                acc[to, :] += lane_groups(half.astype(F32))
            return carry

        return step

    over(1, rows, across(own, 0), 0)
    over(*blocks_of(rest.shape[1]), across(rest, rows), 0)


def own_first_kernel(own, wt_ref, e_ref, cols_ref, zt):
    zt[...] = unit_rows(own[...])[0].astype(BF)

    def body(i):
        e = jnp.exp2(dot(zt[...], wt_ref[i]))
        e_ref[i] = e.astype(BF)
        cols_ref[i] = sublane_groups(e)

    each_step(0, wt_ref.shape[0], body)


def exps_of(side, units, i, wt_ref, e_ref, cols):
    far = units.shape[0]
    height = 384 if far % 384 == 0 else 128

    def down(span, total):
        logits = dot(units[span, :], wt_ref[i])
        for k, at in enumerate(chunks(span)):
            e = jnp.exp2(logits[k * 64 : (k + 1) * 64, :])
            to = pl.ds(pl.multiple_of(side * far + at.start, 64), 64)
            e_ref[i, to, :] = e.astype(BF)
            total = total + sublane_groups(e)
        return total

    return over(far // height, height, down, cols)


def mine_first_kernel(mine, wt_ref, own_cols, e_ref, cols_ref):
    side = lax.axis_index("proto") % 2

    def body(i):
        cols_ref[i] = exps_of(side, mine, i, wt_ref, e_ref, own_cols[i])

    each_step(0, wt_ref.shape[0], body)


def first_kernel(nb, begun, *refs):
    mine, other, wt_ref, own_ref, cols_ref, e_ref, out_ref, acc = refs[begun:]
    rows = own_ref.shape[1]
    side = lax.axis_index("proto") % 2
    acc[...] = jnp.zeros_like(acc)

    def exps(i):
        total = exps_of(1 - side, other, i, wt_ref, e_ref, cols_ref[i])
        if not begun:
            total = exps_of(side, mine, i, wt_ref, e_ref, total)
        return 1.0 / jnp.sum(total, axis=0, keepdims=True)

    refs = (own_ref, e_ref)
    two_steps(wt_ref.shape[0], exps, lambda i, ps: add_across(rows, refs, i, ps, acc))
    for i, row in enumerate(row_sums(nb, rows, acc)):
        out_ref[i : i + 1, :] = row


def start_sweep(nb, sums, cs, turned, acc):
    width = sums.shape[1]
    for i in range(nb):
        scale = 1.0 / sums[i : i + 1]
        span = slice(i * width, (i + 1) * width)
        if i < 2:
            turned[span, :] = jnp.broadcast_to(scale, (LANES, width)).T.astype(BF)
        else:
            cs[:, span] = split_rows(scale)
    acc[...] = jnp.zeros_like(acc)


def proto_scale(refs, i, cs, turned):
    own, rest = refs
    rows = own.shape[1]
    total = jnp.zeros((8, BLK), F32)
    for ref, start in ((own, 0), (rest, rows)):
        for at in chunks(pl.ds(0, rows)):
            scale = turned[start + at.start : start + at.start + 64, :]
            scaled = ref[i, at, :] * jnp.concatenate([scale] * (BLK // LANES), axis=1)
            total = total + sublane_groups((scaled[:32] + scaled[32:]).astype(F32))
    down = dot(cs[:, 2 * rows :], rest[i, rows:, :])
    total = jnp.sum(total, axis=0, keepdims=True) + jnp.sum(down, axis=0, keepdims=True)
    return 1.0 / total


def sweep_kernel(nb, after, x_ref, own_ref, e_ref, out_ref, cs, turned, acc):
    rows = own_ref.shape[1]
    both = (own_ref, e_ref)
    start_sweep(nb, x_ref[...], cs, turned, acc)
    two_steps(
        e_ref.shape[0],
        lambda i: proto_scale(both, i, cs, turned),
        lambda i, ps: add_across(rows, both, i, ps, acc),
    )
    for i, row in enumerate(row_sums(nb, rows, acc)):
        out_ref[i : i + 1, :] = row


def last_sweep_kernel(nb, k, n, hops, chips, x_ref, own_ref, e_ref, ws_rows, student, own_tot, *refs):
    tots, ps_ref, kept, outs = refs[:k], refs[k], refs[k + 1], refs[k + 2 : -5]
    cs, turned, acc, head, grad = refs[-5:]
    rows = own_ref.shape[1]
    both = (own_ref, e_ref)
    start_sweep(nb, x_ref[...], cs, turned, acc)
    grad[...] = jnp.zeros_like(grad)

    def across(i, ps):
        ps_ref[i] = ps
        add_across(rows, both, i, ps, acc)
        grad[...] += dot(own_ref[i] * ps.astype(BF), ws_rows[i])

    two_steps(e_ref.shape[0], lambda i: proto_scale(both, i, cs, turned), across)
    head[...] = jnp.zeros_like(head)
    put_sums(row_sums(nb, rows, acc), head)
    tot = tots[0][...]
    for more in tots[1:]:
        tot = tot + more[...]
    put_sums([own_tot[...]] + [tot[i : i + 1] for i in range(nb - 1)], head, 2 * nb)
    part = rows // n

    def read(r):
        at = pl.ds(pl.multiple_of(r * part, part), part)
        fill = [jnp.zeros((16 - part, grad.shape[1]), F32)] if part < 16 else []
        return jnp.concatenate([grad[at, :], *fill, student[at, :], *fill], axis=0)

    deal(hops, head, read, n, outs, kept, chips)


def deal_kernel(nb, count, hops, *refs):
    k = len(refs) - 3 - len(hops)
    arrived, kept, outs, (head, sums) = refs[:k], refs[k], refs[k + 1 : -2], refs[-2:]
    total = added(arrived)
    head[...] = jnp.zeros_like(head)
    for at in (0, 2 * nb):
        both = joined(total, nb, at)
        put_sums([both[i : i + 1] for i in range(nb)], head, at)
    sums[...] = total[head.shape[0] :]
    size = sums.shape[0] // count

    def read(r):
        return sums[pl.ds(pl.multiple_of(r * size, size), size), :]

    deal(hops, head, read, count, outs, kept)


def own_student_kernel(own, ws_ref, turned_ref, zs_ref, tot_ref, grad, s_ref, acc):
    zs_ref[...] = unit_rows(own[...])[0].astype(BF)
    acc[...] = jnp.zeros_like(acc)
    grad[...] = jnp.zeros_like(grad)
    kept = s_ref.shape[0] > 1

    def body(i):
        s = jnp.exp2(dot(zs_ref[...], ws_ref[i]))
        acc[...] += lane_groups(s)
        s_ref[i if kept else 0] = s.astype(BF)
        grad[...] += dot(s.astype(BF), turned_ref[i])

    each_step(0, ws_ref.shape[0], body)
    tot_ref[...] = row_sums(1, own.shape[0], acc)[0]


def student_kernel(first, count, after, zs_ref, ws_ref, tot_ref, s_ref, acc):
    acc[...] = jnp.zeros_like(acc)
    kept = s_ref.shape[0] > 1
    rows = tot_ref.shape[1]

    def body(i):
        j = i if kept else 0

        def exps(span, carry):
            logits = dot(zs_ref[span, :], ws_ref[i + first])
            for k, at in enumerate(chunks(span)):
                s = jnp.exp2(logits[k * 64 : (k + 1) * 64, :])
                acc[at, :] += lane_groups(s)
                s_ref[j, at, :] = s.astype(BF)
            return carry

        over(zs_ref.shape[0] // rows, rows, exps, 0)

    each_step(0, count, body)
    for i, row in enumerate(row_sums(tot_ref.shape[0], rows, acc)):
        tot_ref[i : i + 1, :] = row


def scaled_features(zs_refs, sums, out):
    here, width = out.shape[0], zs_refs[0].shape[1]
    at = lax.broadcasted_iota(jnp.int32, (here, width), 1)
    row = lax.broadcasted_iota(jnp.int32, (here, width), 0)
    pick = jnp.where(at == row + lax.axis_index("batch") * here, 1.0, 0.0).astype(BF)
    rows = zs_refs[0].shape[0]
    i = 0
    for ref in zs_refs:
        for start in range(0, ref.shape[0], rows):
            turned = lax.dot_general(
                pick,
                ref[start : start + rows, :],
                (((1,), (1,)), ((), ())),
                preferred_element_type=F32,
            )
            out[:, i * rows : (i + 1) * rows] = (turned * (1.0 / sums[i : i + 1])).astype(BF)
            i += 1


def feature_kernel(nb, k, factor, *refs):
    arrived, (feats_ref, own_zs, zs_ref, share_ref, lhs, ratio) = refs[:k], refs[k:]
    part, width = share_ref.shape
    rows = feats_ref.shape[0]
    padded = max(part, 16)
    total = added(arrived)
    sums, tots = joined(total, nb), joined(total, nb, 2 * nb)
    teacher, student = total[-2 * padded :][:part], total[-padded:][:part]
    at = lax.broadcasted_iota(jnp.int32, (part, rows), 1)
    row = lax.broadcasted_iota(jnp.int32, (part, rows), 0)
    pick = at == row + (lax.axis_index("proto") ^ 1) * part
    crop_scale = 1.0 / jnp.sum(jnp.where(pick, sums[0:1], 0.0), axis=1, keepdims=True)
    prob_scale = 1.0 / jnp.sum(jnp.where(pick, tots[0:1], 0.0), axis=1, keepdims=True)
    raw = dot(jnp.where(pick, 1.0, 0.0).astype(BF), feats_ref[...])
    unit, length = unit_rows(raw)
    grad = factor * (student * prob_scale - teacher * crop_scale)
    along = jnp.sum(unit * grad, axis=1, keepdims=True)
    share_ref[...] = ((grad - unit * along) / length).astype(share_ref.dtype)

    scaled_features((own_zs, zs_ref), sums, lhs)
    for i in range(nb):
        span = slice(i * rows, (i + 1) * rows)
        scale = jnp.broadcast_to(sums[i : i + 1] / tots[i : i + 1], (LANES, rows)).T
        ratio[span, :] = scale.astype(BF)


def weight_kernel(first, count, factor, aliased, starts, *refs):
    own_e, e_ref, ps_ref, own_zs, zs_ref, lhs, ratio = refs[1 + aliased : 8 + aliased]
    sources, (out_ref, token, diff, put, sems) = refs[8 + aliased : -5], refs[-5:]
    token[...] = jnp.zeros_like(token)
    rows = own_e.shape[1]

    def copy(i):
        return pltpu.make_async_copy(put.at[i], out_ref.at[:, block(i + first)], sems.at[i])

    def body(i, own_s, s_ref):
        ps = ps_ref[i].astype(BF)

        def down(zs, s, e, start):
            def step(span, acc):
                to = pl.ds(span.start + start, span.size)
                if not starts:
                    diff[to, :] = jnp.exp2(dot(zs[span, :], s[...])).astype(BF)
                for at in chunks(span):
                    to = pl.ds(at.start + start, at.size)
                    scale = jnp.concatenate([ratio[to, :]] * (BLK // LANES), axis=1)
                    left = (s[at, :] if starts else diff[to, :]) * scale
                    diff[to, :] = left - e[i, at, :] * ps
                to = pl.ds(span.start + start, span.size)
                return acc + dot(lhs[:, to], diff[to, :])

            return step

        acc = over(1, rows, down(own_zs, own_s, own_e, 0), jnp.zeros((lhs.shape[0], BLK), F32))
        acc = over(zs_ref.shape[0] // rows, rows, down(zs_ref, s_ref, e_ref, rows), acc)
        put[i - first] = (factor * acc).astype(BF)
        copy(i - first).start()

    def run(low, high, pick):
        if low < high:
            each_step(low, high, lambda i: body(i, *pick(i)))

    if starts:
        own_s, *kept = sources
        for low, high, ref in zip(starts, starts[1:], kept):
            run(
                max(low, first),
                min(high, first + count),
                lambda i, low=low, ref=ref: (own_s.at[i], ref.at[i - low]),
            )
    else:
        run(first, first + count, lambda i: (sources[0].at[i], sources[0].at[i]))
    for i in range(count):
        copy(i).wait()


def join_kernel(hops, after, share, *refs):
    moved, out_ref = refs[:-1], refs[-1]
    rows = share.shape[0]
    me = lax.axis_index("proto") ^ 1
    for hop, ref in zip((0, *hops[::-1]), (share, *moved)):
        place = ((me ^ hop) // hops[0]) % (1 + len(hops))
        out_ref[pl.ds(pl.multiple_of(place * rows, rows), rows), :] = ref[...].astype(out_ref.dtype)


def permute(value, axis, s):
    n = lax.axis_size(axis)
    return lax.ppermute(value, axis, [(i, i ^ s) for i in range(n)])


def stages(n):
    bits = n.bit_length() - 1
    pairs = [[1 << b, 2 << b, 3 << b] if b + 1 < bits else [1 << b] for b in range(1, bits, 2)]
    return [[1]] + pairs


def permutes(value, axis, hops):
    return [permute(value, axis, hop) for hop in reversed(hops)][::-1]


def crossed(hop):
    return hop | 1


def shards(teacher_feats, student_feats, teacher_weight, student_weight):
    rows, width = teacher_feats.shape
    protos = teacher_weight.shape[1]
    nb, n = lax.axis_size("batch"), lax.axis_size("proto")
    crops, protos_all = rows * nb, protos * n
    here, part = width // nb, rows // n
    padded = max(part, 16)
    large = -(-4 * nb // 16) * 16
    keep = crops * protos <= 8 * MIB
    big = crops * protos
    wide = width * protos
    steps = protos // BLK

    limit = (16 if keep else 56) * MIB

    vmem = pl.BlockSpec(memory_space=pltpu.VMEM)
    hbm = pl.BlockSpec(memory_space=pltpu.HBM)
    anywhere = pl.BlockSpec(memory_space=pl.ANY)

    def shape(*dims, dtype=F32):
        return jax.ShapeDtypeStruct(dims, dtype)

    def call(kernel, out_shape, scratch, flops, moved, exps, *args, far=(), after=(), aliases={}):
        far = [pltpu.with_memory_space_constraint(a, pltpu.HBM) for a in far]
        return pl.pallas_call(
            kernel,
            out_shape=out_shape,
            in_specs=[hbm] * len(far)
            + [anywhere] * len(after)
            + [vmem] * len(args),
            out_specs=[vmem] * len(out_shape),
            scratch_shapes=scratch,
            input_output_aliases=aliases,
            compiler_params=pltpu.CompilerParams(vmem_limit_bytes=limit),
            cost_estimate=pl.CostEstimate(
                flops=int(flops), bytes_accessed=int(moved), transcendentals=int(exps)
            ),
        )(*far, *after, *args)

    def weight_call(kernel, out_shape, scratch, flops, moved, done, after, *args):
        return pl.pallas_call(
            kernel,
            out_shape=[out_shape, shape(8, LANES)],
            in_specs=[hbm] * len(done) + [anywhere] + [vmem] * len(args),
            out_specs=[hbm, vmem],
            scratch_shapes=scratch,
            input_output_aliases={0: 0} if done else {},
            compiler_params=pltpu.CompilerParams(vmem_limit_bytes=limit),
            cost_estimate=pl.CostEstimate(
                flops=int(flops), bytes_accessed=int(moved), transcendentals=0
            ),
        )(*done, after, *args)

    rest, half = crops - rows, rows // 2
    turned_crops = pltpu.VMEM((16, crops), BF)
    lane_sums = pltpu.VMEM((crops, LANES), F32)
    rounds = stages(n)
    sizes = [steps // 4, steps - steps // 4]
    weight_sizes = [steps // 4, steps - steps // 4]

    (mine,) = call(
        halves_kernel,
        [shape(half * 3 // 2, width, dtype=BF)],
        [pltpu.SemaphoreType.DMA((2,))],
        0,
        4 * rows * width,
        0,
        far=(teacher_feats, student_feats),
    )
    blocks = permutes(mine, "batch", range(1, nb))

    unit_wt, unit_ws, turned_ws = call(
        weights_kernel,
        [shape(steps, width, BLK, dtype=BF)] * 2 + [shape(steps, BLK, width, dtype=BF)],
        [pltpu.VMEM((2, steps, width, BLK), BF), pltpu.SemaphoreType.DMA((2, steps))],
        16 * wide,
        10 * wide,
        0,
        far=(teacher_weight, student_weight),
    )
    own_e, own_cols = call(
        own_first_kernel,
        [shape(steps, rows, BLK, dtype=BF), shape(steps, 8, BLK)],
        [pltpu.VMEM((rows, width), BF)],
        2 * rows * protos * width,
        2 * rows * protos,
        rows * protos,
        teacher_feats,
        unit_wt,
    )
    own_zs, own_tot, grad, own_s = call(
        own_student_kernel,
        [
            shape(rows, width, dtype=BF),
            shape(1, rows),
            shape(rows, width),
            shape(steps if keep else 1, rows, BLK, dtype=BF),
        ],
        [pltpu.VMEM((rows, LANES), F32)],
        4 * rows * protos * width,
        2 * rows * protos,
        rows * protos,
        student_feats,
        unit_ws,
        turned_ws,
    )

    mine, quarters = call(
        units_kernel,
        [shape(rest // 2, width, dtype=BF), shape(rest // 4, width, dtype=BF)],
        [],
        8 * crops * width,
        2 * crops * width,
        0,
        *reversed(blocks),
        after=(own_cols, own_tot),
    )
    other = permute(mine, "proto", 1)
    moved = permute(quarters, "proto", 2)

    begun, cols = (), own_cols
    if keep:
        *begun, cols = call(
            mine_first_kernel,
            [shape(steps, rest, BLK, dtype=BF), shape(steps, 8, BLK)],
            [],
            rest * protos * width,
            rest * protos,
            rest * protos // 2,
            mine,
            unit_wt,
            own_cols,
        )
    e, x = call(
        functools.partial(first_kernel, nb, len(begun)),
        [shape(steps, rest, BLK, dtype=BF), shape(nb, width)],
        [lane_sums],
        2 * big * width,
        2 * big,
        big,
        *begun,
        mine,
        other,
        unit_wt,
        own_e,
        cols,
        aliases={0: 0} if begun else {},
    )
    (student_mine,) = call(
        functools.partial(quarters_kernel, half // 2),
        [shape(rest // 2, width, dtype=BF)],
        [],
        0,
        2 * rest * width,
        0,
        quarters,
        moved,
        after=(x,),
    )
    (zs,) = call(
        place_kernel,
        [shape(rest, width, dtype=BF)],
        [],
        0,
        4 * rest * width,
        0,
        student_mine,
        permute(student_mine, "proto", 1),
    )

    tots, kept = [], []

    def student_piece(after):
        k = len(kept)
        tot, piece = call(
            functools.partial(student_kernel, sum(sizes[:k]), sizes[k]),
            [shape(nb - 1, rows), shape(sizes[k] if keep else 1, rest, BLK, dtype=BF)],
            [pltpu.VMEM((rest, LANES), F32)],
            2 * rest * width * BLK * sizes[k],
            2 * rest * BLK * sizes[k],
            rest * BLK * sizes[k],
            zs,
            unit_ws,
            after=(after,),
        )
        tots.append(tot)
        kept.append(piece)

    def summed(x, pieces):
        for k, hops in enumerate(rounds):
            moved = permutes(x, "proto", [crossed(hop) for hop in hops])
            if k in pieces:
                student_piece(x)
            for value in reversed(moved):
                x = x + value
        return x

    x = summed(x, ())
    (x,) = call(
        functools.partial(sweep_kernel, nb),
        [shape(nb, width)],
        [turned_crops, pltpu.VMEM((2 * rows, LANES), BF), lane_sums],
        4 * big,
        2 * big,
        0,
        x,
        own_e,
        e,
        after=(zs,),
    )
    x = summed(x, (0, 1))

    def dealt(count, many):
        height = large + count // many * 2 * padded
        return [shape(height, width)] + [shape(height, width, dtype=BF)] * (many - 1)

    scale, *x = call(
        functools.partial(last_sweep_kernel, nb, len(tots), n, rounds[0], 1 + len(rounds[1])),
        [shape(steps, 1, BLK)] + dealt(n, 1 + len(rounds[0])),
        [
            turned_crops,
            pltpu.VMEM((2 * rows, LANES), BF),
            lane_sums,
            pltpu.VMEM((large, width), F32),
            pltpu.VMEM((rows, width), F32),
        ],
        4 * big,
        2 * big,
        0,
        x,
        own_e,
        e,
        turned_ws,
        grad,
        own_tot,
        *tots,
    )
    count = n
    for k, hops in enumerate(rounds):
        pairs = [crossed(hop) if k == 1 else hop for hop in hops]
        moved = [permute(x[1 + i], "proto", pairs[i]) for i in reversed(range(len(pairs)))]
        x = [x[0]] + moved
        count //= 1 + len(hops)
        if k + 1 < len(rounds):
            x = call(
                functools.partial(deal_kernel, nb, count, rounds[k + 1]),
                dealt(count, 1 + len(rounds[k + 1])),
                [pltpu.VMEM((large, width), F32), pltpu.VMEM((count * 2 * padded, width), F32)],
                4 * count * padded * width,
                8 * count * padded * width,
                0,
                *x,
            )

    factor = protos_all * math.sqrt(width / protos_all) * (student_temp / LOG2E)
    share, lhs, ratio = call(
        functools.partial(feature_kernel, nb, len(x), factor),
        [
            shape(part, width, dtype=BF if part % 16 == 0 else F32),
            shape(here, crops, dtype=BF),
            shape(crops, LANES, dtype=BF),
        ],
        [],
        0,
        8 * rows * width,
        0,
        *x,
        student_feats,
        own_zs,
        zs,
    )

    done = ()
    for k, hops in enumerate(rounds):
        moved = permutes(share, "proto", [crossed(hop) for hop in hops])
        if k < len(weight_sizes):
            first, size = sum(weight_sizes[:k]), weight_sizes[k]
            *done, token = weight_call(
                functools.partial(
                    weight_kernel,
                    first,
                    size,
                    protos_all * math.sqrt(width / crops),
                    len(done),
                    [sum(sizes[:i]) for i in range(len(sizes) + 1)] if keep else [],
                ),
                shape(here, protos, dtype=BF),
                [
                    pltpu.VMEM((crops, BLK), BF),
                    pltpu.VMEM((size, here, BLK), BF),
                    pltpu.SemaphoreType.DMA((size,)),
                ],
                2 * big * here * size // steps,
                4 * big * size // steps,
                done,
                share,
                own_e,
                e,
                scale,
                own_zs,
                zs,
                lhs,
                ratio,
                *((own_s, *kept) if keep else (unit_ws,)),
            )
        (share,) = call(
            functools.partial(join_kernel, hops),
            [shape((1 + len(hops)) * share.shape[0], width, dtype=BF if k + 1 == len(rounds) else share.dtype)],
            [],
            0,
            8 * share.shape[0] * width,
            0,
            share,
            *reversed(moved),
            after=(token,),
        )
    return (done[0], share)


def solution(mesh):
    return jax.shard_map(
        shards,
        mesh=mesh,
        in_specs=(P("batch", None), P("batch", None), P(None, "proto"), P(None, "proto")),
        out_specs=(P("batch", "proto"), P("batch", None)),
        check_vma=False,
    )
```

```python
import functools
import math

import jax
import jax.numpy as jnp
from jax import lax
from jax.experimental import pallas as pl
from jax.experimental.pallas import tpu as pltpu
from jax.sharding import PartitionSpec as P

ITERS = 3

teacher_temp = 0.07
student_temp = 0.1
epsilon = 1e-06
LOG2E = 1.4426950408889634
BF = jnp.bfloat16
F32 = jnp.float32
MIB = 1024 * 1024
BLK = 512
LANES = 128


def dot(a, b):
    return jnp.dot(a, b, preferred_element_type=F32)


def split(values):
    high = values.astype(BF).astype(F32)
    return high, (values - high).astype(BF).astype(F32)


def split_rows(row):
    high, low = split(row)
    at = lax.broadcasted_iota(jnp.int32, (16, row.shape[1]), 0)
    return jnp.where(at == 0, high, jnp.where(at == 1, low, 0.0)).astype(BF)


def unit_rows(raw):
    values = raw.astype(F32)
    length = jnp.sqrt(jnp.sum(values * values, axis=1, keepdims=True) + epsilon)
    return values / length, length


def over(count, size, body, carry):
    if count <= 4:
        for i in range(count):
            carry = body(pl.ds(i * size, size), carry)
        return carry

    def step(i, carry):
        return body(pl.ds(pl.multiple_of(i * size, size), size), carry)

    return lax.fori_loop(0, count, step, carry)


def chunks(span):
    for at in range(0, span.size, 64):
        start = span.start + at
        yield pl.ds(start if isinstance(start, int) else pl.multiple_of(start, 64), 64)


def block(i):
    return pl.ds(pl.multiple_of(i * BLK, BLK), BLK)


def each_step(low, high, body):
    for i in range(low, high):
        body(i)


def in_turn(left, right):
    done = 0
    for k, run in enumerate(left):
        run()
        while done * len(left) < (k + 1) * len(right):
            right[done]()
            done += 1


def two_steps(steps, first, second):
    runs, result = first(0)
    in_turn(runs, [])
    for i in range(1, steps):
        carry = result()
        runs, result = first(i)
        in_turn(second(i - 1, carry), runs)
    in_turn(second(steps - 1, result()), [])


def lane_groups(values):
    out = values[:, :LANES]
    for at in range(LANES, values.shape[1], LANES):
        out = out + values[:, at : at + LANES]
    return out


def sublane_groups(values):
    return jnp.sum(values.reshape(-1, 8, values.shape[1]), axis=0)


def joined(total, nb, at=0):
    return total[at : at + nb] + total[at + nb : at + 2 * nb]


def blocks_of(crops):
    height = next(h for h in (768, 512, 256, crops) if crops % h == 0)
    return crops // height, height


def row_sums(nb, rows, acc, at=0):
    spans = [slice(at + i * rows, at + (i + 1) * rows) for i in range(nb)]
    return [jnp.sum(acc[span, :].T, axis=0, keepdims=True) for span in spans]


def put_sums(sums, out, at=0):
    for i, row in enumerate(sums):
        high, low = split(row)
        out[at + i : at + i + 1, :] = high
        out[at + len(sums) + i : at + len(sums) + i + 1, :] = low


def deal(hops, head, read, count, outs, kept, chips=0):
    many = 1 + len(hops)
    me = lax.axis_index("proto")
    digit = (me // hops[0]) % many
    for hop, out in zip((0, *hops), (kept, *outs)):
        out[0 : head.shape[0], :] = head[...].astype(out.dtype)
        for m in range(count // many):
            turn = (me // 2 % chips == m % chips).astype(jnp.int32) if chips else 0
            rows = read(m * many + (digit ^ (hop // hops[0]) ^ turn)).astype(out.dtype)
            at = head.shape[0] + m * rows.shape[0]
            out[at : at + rows.shape[0], :] = rows


def added(refs):
    acc = refs[0][...].astype(F32)
    for ref in refs[1:]:
        acc = acc + ref[...].astype(F32)
    return acc


def halves_kernel(teacher_ref, student_ref, out, sems):
    half = out.shape[0] * 2 // 3
    me = lax.axis_index("proto")
    start = pl.multiple_of(me % 2 * half, half)
    quarter = pl.multiple_of(start + me // 2 % 2 * (half // 2), half // 2)
    first = pltpu.make_async_copy(
        teacher_ref.at[pl.ds(start, half), :], out.at[0:half, :], sems.at[0]
    )
    second = pltpu.make_async_copy(
        student_ref.at[pl.ds(quarter, half // 2), :], out.at[half:, :], sems.at[1]
    )
    first.start()
    second.start()
    first.wait()
    second.wait()


def units_kernel(after, also, *refs):
    blocks, outs = refs[:-2], refs[-2:]
    start = 0
    for out in outs:
        size = out.shape[0] // len(blocks)
        for i, ref in enumerate(blocks):
            rows = unit_rows(ref[start : start + size, :])[0]
            out[i * size : (i + 1) * size, :] = rows.astype(BF)
        start += size


def quarters_kernel(size, after, mine, moved, out):
    side = lax.axis_index("proto") // 2 % 2
    for i in range(mine.shape[0] // size):
        for ref, place in ((mine, side), (moved, 1 - side)):
            at = pl.multiple_of((2 * i + place) * size, size)
            out[pl.ds(at, size), :] = ref[i * size : (i + 1) * size, :]


def place_kernel(mine, other, out):
    far = mine.shape[0]
    core = lax.axis_index("proto") % 2
    for ref, place in ((mine, core), (other, 1 - core)):
        out[pl.ds(pl.multiple_of(place * far, 128), far), :] = ref[...]


def weights_kernel(wt_ref, ws_ref, wt_out, ws_out, turned_out, raw, sems):
    steps = wt_out.shape[0]

    def copy(i, which):
        src = (wt_ref, ws_ref)[which]
        return pltpu.make_async_copy(src.at[:, block(i)], raw.at[which, i], sems.at[which, i])

    for which in range(2):
        for i in range(steps):
            copy(i, which).start()

    def unit(i, which):
        copy(i, which).wait()
        values = raw[which, i].astype(F32)
        length = jnp.sqrt(jnp.sum(values * values, axis=0, keepdims=True) + epsilon)
        return (values * ((LOG2E / (teacher_temp, student_temp)[which]) / length)).astype(BF)

    def teacher(i):
        wt_out[i] = unit(i, 0)

    def student(i):
        ws = unit(i, 1)
        ws_out[i] = ws
        turned_out[i] = ws.T

    each_step(0, steps, teacher)
    each_step(0, steps, student)


def add_across(rows, refs, i, ps, acc):
    own, rest = refs
    ps = ps.astype(BF)

    def add(ref, at, to):
        scaled = ref[i, at, :] * ps
        half = scaled[:, : BLK // 2] + scaled[:, BLK // 2 :]
        acc[to, :] += lane_groups(half.astype(F32))

    def many():
        def step(span, carry):
            for at in chunks(span):
                add(rest, at, pl.ds(at.start + rows, at.size))
            return carry

        over(*blocks_of(rest.shape[1]), step, 0)

    runs = [functools.partial(add, own, at, at) for at in chunks(pl.ds(0, rows))]
    if rest.shape[1] > 1024:
        return runs + [many]
    for at in chunks(pl.ds(0, rest.shape[1])):
        runs.append(functools.partial(add, rest, at, pl.ds(at.start + rows, at.size)))
    return runs


def own_first_kernel(own, wt_ref, e_ref, cols_ref, zt):
    zt[...] = unit_rows(own[...])[0].astype(BF)

    def body(i):
        e = jnp.exp2(dot(zt[...], wt_ref[i]))
        e_ref[i] = e.astype(BF)
        cols_ref[i] = sublane_groups(e)

    each_step(0, wt_ref.shape[0], body)


def exps_of(side, units, i, wt_ref, e_ref, cell):
    far = units.shape[0]
    height = 384 if far % 384 == 0 else 128
    logits = [None]

    def multiply(span):
        logits[0] = dot(units[span, :], wt_ref[i])

    def put(k, start):
        e = jnp.exp2(logits[0][k * 64 : (k + 1) * 64, :])
        e_ref[i, pl.ds(pl.multiple_of(side * far + start, 64), 64), :] = e.astype(BF)
        cell[0] = cell[0] + sublane_groups(e)

    def step(span, total):
        cell[0] = total
        multiply(span)
        for k, at in enumerate(chunks(span)):
            put(k, at.start)
        return cell[0]

    def many():
        cell[0] = over(far // height, height, step, cell[0])

    if far > height:
        return [many]
    runs = [functools.partial(multiply, pl.ds(0, far))]
    return runs + [functools.partial(put, k, k * 64) for k in range(far // 64)]


def mine_first_kernel(mine, wt_ref, own_cols, e_ref, cols_ref):
    side = lax.axis_index("proto") % 2

    def body(i):
        cell = [own_cols[i]]
        in_turn(exps_of(side, mine, i, wt_ref, e_ref, cell), [])
        cols_ref[i] = cell[0]

    each_step(0, wt_ref.shape[0], body)


def first_kernel(nb, begun, *refs):
    mine, other, wt_ref, own_ref, cols_ref, quarters, e_ref, out_ref, passed, acc = refs[begun:]
    passed[...] = quarters[...]
    rows = own_ref.shape[1]
    side = lax.axis_index("proto") % 2
    acc[...] = jnp.zeros_like(acc)

    def exps(i):
        cell = [cols_ref[i]]
        runs = exps_of(1 - side, other, i, wt_ref, e_ref, cell)
        if not begun:
            runs = runs + exps_of(side, mine, i, wt_ref, e_ref, cell)
        return runs, lambda: 1.0 / jnp.sum(cell[0], axis=0, keepdims=True)

    refs = (own_ref, e_ref)
    two_steps(wt_ref.shape[0], exps, lambda i, ps: add_across(rows, refs, i, ps, acc))
    for i, row in enumerate(row_sums(nb, rows, acc)):
        out_ref[i : i + 1, :] = row


def start_sweep(nb, sums, cs, turned, acc):
    width = sums.shape[1]
    for i in range(nb):
        scale = 1.0 / sums[i : i + 1]
        span = slice(i * width, (i + 1) * width)
        if i < 2:
            turned[span, :] = jnp.broadcast_to(scale, (LANES, width)).T.astype(BF)
        else:
            cs[:, span] = split_rows(scale)
    acc[...] = jnp.zeros_like(acc)


def proto_scale(refs, i, cs, turned):
    own, rest = refs
    rows = own.shape[1]
    cell, down = [jnp.zeros((8, BLK), F32)], [None]

    def multiply():
        down[0] = dot(cs[:, 2 * rows :], rest[i, rows:, :])

    def add(ref, start, at):
        scale = turned[start + at.start : start + at.start + 64, :]
        scaled = ref[i, at, :] * jnp.concatenate([scale] * (BLK // LANES), axis=1)
        cell[0] = cell[0] + sublane_groups((scaled[:32] + scaled[32:]).astype(F32))

    runs = [multiply]
    for ref, start in ((own, 0), (rest, rows)):
        runs += [functools.partial(add, ref, start, at) for at in chunks(pl.ds(0, rows))]

    def result():
        total = jnp.sum(cell[0], axis=0, keepdims=True) + jnp.sum(down[0], axis=0, keepdims=True)
        return 1.0 / total

    return runs, result


def sweep_kernel(nb, after, x_ref, own_ref, e_ref, out_ref, cs, turned, acc):
    rows = own_ref.shape[1]
    both = (own_ref, e_ref)
    start_sweep(nb, x_ref[...], cs, turned, acc)
    two_steps(
        e_ref.shape[0],
        lambda i: proto_scale(both, i, cs, turned),
        lambda i, ps: add_across(rows, both, i, ps, acc),
    )
    for i, row in enumerate(row_sums(nb, rows, acc)):
        out_ref[i : i + 1, :] = row


def last_sweep_kernel(nb, k, n, hops, chips, x_ref, own_ref, e_ref, ws_rows, student, own_tot, *refs):
    tots, ps_ref, kept, outs = refs[:k], refs[k], refs[k + 1], refs[k + 2 : -5]
    cs, turned, acc, head, grad = refs[-5:]
    rows = own_ref.shape[1]
    both = (own_ref, e_ref)
    start_sweep(nb, x_ref[...], cs, turned, acc)
    grad[...] = jnp.zeros_like(grad)

    def across(i, ps):
        def add_grad():
            ps_ref[i] = ps
            grad[...] += dot(own_ref[i] * ps.astype(BF), ws_rows[i])

        return [add_grad] + add_across(rows, both, i, ps, acc)

    two_steps(e_ref.shape[0], lambda i: proto_scale(both, i, cs, turned), across)
    head[...] = jnp.zeros_like(head)
    put_sums(row_sums(nb, rows, acc), head)
    tot = tots[0][...]
    for more in tots[1:]:
        tot = tot + more[...]
    put_sums([own_tot[...]] + [tot[i : i + 1] for i in range(nb - 1)], head, 2 * nb)
    part = rows // n

    def read(r):
        at = pl.ds(pl.multiple_of(r * part, part), part)
        fill = [jnp.zeros((16 - part, grad.shape[1]), F32)] if part < 16 else []
        return jnp.concatenate([grad[at, :], *fill, student[at, :], *fill], axis=0)

    deal(hops, head, read, n, outs, kept, chips)


def deal_kernel(nb, count, hops, *refs):
    k = len(refs) - 3 - len(hops)
    arrived, kept, outs, (head, sums) = refs[:k], refs[k], refs[k + 1 : -2], refs[-2:]
    total = added(arrived)
    head[...] = jnp.zeros_like(head)
    for at in (0, 2 * nb):
        both = joined(total, nb, at)
        put_sums([both[i : i + 1] for i in range(nb)], head, at)
    sums[...] = total[head.shape[0] :]
    size = sums.shape[0] // count

    def read(r):
        return sums[pl.ds(pl.multiple_of(r * size, size), size), :]

    deal(hops, head, read, count, outs, kept)


def own_student_kernel(own, ws_ref, turned_ref, zs_ref, tot_ref, grad, s_ref, acc):
    zs_ref[...] = unit_rows(own[...])[0].astype(BF)
    acc[...] = jnp.zeros_like(acc)
    grad[...] = jnp.zeros_like(grad)
    kept = s_ref.shape[0] > 1

    def body(i):
        s = jnp.exp2(dot(zs_ref[...], ws_ref[i]))
        acc[...] += lane_groups(s)
        s_ref[i if kept else 0] = s.astype(BF)
        grad[...] += dot(s.astype(BF), turned_ref[i])

    each_step(0, ws_ref.shape[0], body)
    tot_ref[...] = row_sums(1, own.shape[0], acc)[0]


def student_kernel(first, count, after, zs_ref, ws_ref, tot_ref, s_ref, acc):
    acc[...] = jnp.zeros_like(acc)
    kept = s_ref.shape[0] > 1
    rows = tot_ref.shape[1]

    def body(i):
        j = i if kept else 0

        def exps(span, carry):
            logits = dot(zs_ref[span, :], ws_ref[i + first])
            for k, at in enumerate(chunks(span)):
                s = jnp.exp2(logits[k * 64 : (k + 1) * 64, :])
                acc[at, :] += lane_groups(s)
                s_ref[j, at, :] = s.astype(BF)
            return carry

        over(zs_ref.shape[0] // rows, rows, exps, 0)

    each_step(0, count, body)
    for i, row in enumerate(row_sums(tot_ref.shape[0], rows, acc)):
        tot_ref[i : i + 1, :] = row


def scaled_features(zs_refs, sums, out):
    here, width = out.shape[0], zs_refs[0].shape[1]
    at = lax.broadcasted_iota(jnp.int32, (here, width), 1)
    row = lax.broadcasted_iota(jnp.int32, (here, width), 0)
    pick = jnp.where(at == row + lax.axis_index("batch") * here, 1.0, 0.0).astype(BF)
    rows = zs_refs[0].shape[0]
    i = 0
    for ref in zs_refs:
        for start in range(0, ref.shape[0], rows):
            turned = lax.dot_general(
                pick,
                ref[start : start + rows, :],
                (((1,), (1,)), ((), ())),
                preferred_element_type=F32,
            )
            out[:, i * rows : (i + 1) * rows] = (turned * (1.0 / sums[i : i + 1])).astype(BF)
            i += 1


def feature_kernel(nb, k, factor, *refs):
    arrived, (feats_ref, own_zs, zs_ref, share_ref, lhs, ratio) = refs[:k], refs[k:]
    part, width = share_ref.shape
    rows = feats_ref.shape[0]
    padded = max(part, 16)
    total = added(arrived)
    sums, tots = joined(total, nb), joined(total, nb, 2 * nb)
    teacher, student = total[-2 * padded :][:part], total[-padded:][:part]
    at = lax.broadcasted_iota(jnp.int32, (part, rows), 1)
    row = lax.broadcasted_iota(jnp.int32, (part, rows), 0)
    pick = at == row + (lax.axis_index("proto") ^ 1) * part
    crop_scale = 1.0 / jnp.sum(jnp.where(pick, sums[0:1], 0.0), axis=1, keepdims=True)
    prob_scale = 1.0 / jnp.sum(jnp.where(pick, tots[0:1], 0.0), axis=1, keepdims=True)
    raw = dot(jnp.where(pick, 1.0, 0.0).astype(BF), feats_ref[...])
    unit, length = unit_rows(raw)
    grad = factor * (student * prob_scale - teacher * crop_scale)
    along = jnp.sum(unit * grad, axis=1, keepdims=True)
    share_ref[...] = ((grad - unit * along) / length).astype(share_ref.dtype)

    scaled_features((own_zs, zs_ref), sums, lhs)
    for i in range(nb):
        span = slice(i * rows, (i + 1) * rows)
        scale = jnp.broadcast_to(sums[i : i + 1] / tots[i : i + 1], (LANES, rows)).T
        ratio[span, :] = scale.astype(BF)


def weight_kernel(first, count, factor, aliased, starts, *refs):
    own_e, e_ref, ps_ref, own_zs, zs_ref, lhs, ratio = refs[1 + aliased : 8 + aliased]
    sources, (out_ref, token, diff, put, sems) = refs[8 + aliased : -5], refs[-5:]
    token[...] = jnp.zeros_like(token)
    rows = own_e.shape[1]

    def copy(i):
        return pltpu.make_async_copy(put.at[i], out_ref.at[:, block(i + first)], sems.at[i])

    def body(i, own_s, s_ref):
        ps = ps_ref[i].astype(BF)

        def down(zs, s, e, start):
            def step(span, acc):
                to = pl.ds(span.start + start, span.size)
                if not starts:
                    diff[to, :] = jnp.exp2(dot(zs[span, :], s[...])).astype(BF)
                for at in chunks(span):
                    to = pl.ds(at.start + start, at.size)
                    scale = jnp.concatenate([ratio[to, :]] * (BLK // LANES), axis=1)
                    left = (s[at, :] if starts else diff[to, :]) * scale
                    diff[to, :] = left - e[i, at, :] * ps
                to = pl.ds(span.start + start, span.size)
                return acc + dot(lhs[:, to], diff[to, :])

            return step

        acc = over(1, rows, down(own_zs, own_s, own_e, 0), jnp.zeros((lhs.shape[0], BLK), F32))
        acc = over(zs_ref.shape[0] // rows, rows, down(zs_ref, s_ref, e_ref, rows), acc)
        put[i - first] = (factor * acc).astype(BF)
        copy(i - first).start()

    def run(low, high, pick):
        if low < high:
            each_step(low, high, lambda i: body(i, *pick(i)))

    if starts:
        own_s, *kept = sources
        for low, high, ref in zip(starts, starts[1:], kept):
            run(
                max(low, first),
                min(high, first + count),
                lambda i, low=low, ref=ref: (own_s.at[i], ref.at[i - low]),
            )
    else:
        run(first, first + count, lambda i: (sources[0].at[i], sources[0].at[i]))
    for i in range(count):
        copy(i).wait()


def join_kernel(hops, after, share, *refs):
    moved, out_ref = refs[:-1], refs[-1]
    rows = share.shape[0]
    me = lax.axis_index("proto") ^ 1
    for hop, ref in zip((0, *hops), (share, *moved)):
        place = ((me ^ hop) // hops[0]) % (1 + len(hops))
        out_ref[pl.ds(pl.multiple_of(place * rows, rows), rows), :] = ref[...].astype(out_ref.dtype)


def permute(value, axis, s):
    n = lax.axis_size(axis)
    return lax.ppermute(value, axis, [(i, i ^ s) for i in range(n)])


def stages(n):
    bits = n.bit_length() - 1
    pairs = [[1 << b, 2 << b, 3 << b] if b + 1 < bits else [1 << b] for b in range(1, bits, 2)]
    return [[1]] + pairs


def permutes(value, axis, hops):
    return [permute(value, axis, hop) for hop in reversed(hops)][::-1]


def crossed(hop):
    return hop | 1


def shards(teacher_feats, student_feats, teacher_weight, student_weight):
    rows, width = teacher_feats.shape
    protos = teacher_weight.shape[1]
    nb, n = lax.axis_size("batch"), lax.axis_size("proto")
    crops, protos_all = rows * nb, protos * n
    here, part = width // nb, rows // n
    padded = max(part, 16)
    large = -(-4 * nb // 16) * 16
    keep = crops * protos <= 8 * MIB
    big = crops * protos
    wide = width * protos
    steps = protos // BLK

    limit = (16 if keep else 56) * MIB

    vmem = pl.BlockSpec(memory_space=pltpu.VMEM)
    hbm = pl.BlockSpec(memory_space=pltpu.HBM)
    anywhere = pl.BlockSpec(memory_space=pl.ANY)

    def shape(*dims, dtype=F32):
        return jax.ShapeDtypeStruct(dims, dtype)

    def call(kernel, out_shape, scratch, flops, moved, exps, *args, far=(), after=(), aliases={}):
        far = [pltpu.with_memory_space_constraint(a, pltpu.HBM) for a in far]
        return pl.pallas_call(
            kernel,
            out_shape=out_shape,
            in_specs=[hbm] * len(far)
            + [anywhere] * len(after)
            + [vmem] * len(args),
            out_specs=[vmem] * len(out_shape),
            scratch_shapes=scratch,
            input_output_aliases=aliases,
            compiler_params=pltpu.CompilerParams(vmem_limit_bytes=limit),
            cost_estimate=pl.CostEstimate(
                flops=int(flops), bytes_accessed=int(moved), transcendentals=int(exps)
            ),
        )(*far, *after, *args)

    def weight_call(kernel, out_shape, scratch, flops, moved, done, after, *args):
        return pl.pallas_call(
            kernel,
            out_shape=[out_shape, shape(8, LANES)],
            in_specs=[hbm] * len(done) + [anywhere] + [vmem] * len(args),
            out_specs=[hbm, vmem],
            scratch_shapes=scratch,
            input_output_aliases={0: 0} if done else {},
            compiler_params=pltpu.CompilerParams(vmem_limit_bytes=limit),
            cost_estimate=pl.CostEstimate(
                flops=int(flops), bytes_accessed=int(moved), transcendentals=0
            ),
        )(*done, after, *args)

    rest, half = crops - rows, rows // 2
    turned_crops = pltpu.VMEM((16, crops), BF)
    lane_sums = pltpu.VMEM((crops, LANES), F32)
    rounds = stages(n)
    sizes = [steps // 4, steps - steps // 4]
    weight_sizes = [steps // 4, steps - steps // 4]

    (mine,) = call(
        halves_kernel,
        [shape(half * 3 // 2, width, dtype=BF)],
        [pltpu.SemaphoreType.DMA((2,))],
        0,
        4 * rows * width,
        0,
        far=(teacher_feats, student_feats),
    )
    blocks = permutes(mine, "batch", range(1, nb))

    unit_wt, unit_ws, turned_ws = call(
        weights_kernel,
        [shape(steps, width, BLK, dtype=BF)] * 2 + [shape(steps, BLK, width, dtype=BF)],
        [pltpu.VMEM((2, steps, width, BLK), BF), pltpu.SemaphoreType.DMA((2, steps))],
        16 * wide,
        10 * wide,
        0,
        far=(teacher_weight, student_weight),
    )
    own_e, own_cols = call(
        own_first_kernel,
        [shape(steps, rows, BLK, dtype=BF), shape(steps, 8, BLK)],
        [pltpu.VMEM((rows, width), BF)],
        2 * rows * protos * width,
        2 * rows * protos,
        rows * protos,
        teacher_feats,
        unit_wt,
    )
    own_zs, own_tot, grad, own_s = call(
        own_student_kernel,
        [
            shape(rows, width, dtype=BF),
            shape(1, rows),
            shape(rows, width),
            shape(steps if keep else 1, rows, BLK, dtype=BF),
        ],
        [pltpu.VMEM((rows, LANES), F32)],
        4 * rows * protos * width,
        2 * rows * protos,
        rows * protos,
        student_feats,
        unit_ws,
        turned_ws,
    )

    mine, quarters = call(
        units_kernel,
        [shape(rest // 2, width, dtype=BF), shape(rest // 4, width, dtype=BF)],
        [],
        8 * crops * width,
        2 * crops * width,
        0,
        *blocks,
        after=(own_cols, own_tot),
    )
    other = permute(mine, "proto", 1)

    begun, cols = (), own_cols
    if keep:
        *begun, cols = call(
            mine_first_kernel,
            [shape(steps, rest, BLK, dtype=BF), shape(steps, 8, BLK)],
            [],
            rest * protos * width,
            rest * protos,
            rest * protos // 2,
            mine,
            unit_wt,
            own_cols,
        )
    e, x, quarters = call(
        functools.partial(first_kernel, nb, len(begun)),
        [
            shape(steps, rest, BLK, dtype=BF),
            shape(nb, width),
            shape(rest // 4, width, dtype=BF),
        ],
        [lane_sums],
        2 * big * width,
        2 * big,
        big,
        *begun,
        mine,
        other,
        unit_wt,
        own_e,
        cols,
        quarters,
        aliases={0: 0} if begun else {},
    )
    (student_mine,) = call(
        functools.partial(quarters_kernel, half // 2),
        [shape(rest // 2, width, dtype=BF)],
        [],
        0,
        2 * rest * width,
        0,
        quarters,
        permute(quarters, "proto", 2),
        after=(x,),
    )
    (zs,) = call(
        place_kernel,
        [shape(rest, width, dtype=BF)],
        [],
        0,
        4 * rest * width,
        0,
        student_mine,
        permute(student_mine, "proto", 1),
    )

    tots, kept = [], []

    def student_piece(after):
        k = len(kept)
        tot, piece = call(
            functools.partial(student_kernel, sum(sizes[:k]), sizes[k]),
            [shape(nb - 1, rows), shape(sizes[k] if keep else 1, rest, BLK, dtype=BF)],
            [pltpu.VMEM((rest, LANES), F32)],
            2 * rest * width * BLK * sizes[k],
            2 * rest * BLK * sizes[k],
            rest * BLK * sizes[k],
            zs,
            unit_ws,
            after=(after,),
        )
        tots.append(tot)
        kept.append(piece)

    def summed(x, pieces):
        for k, hops in enumerate(rounds):
            moved = permutes(x, "proto", [crossed(hop) for hop in hops])
            if k in pieces:
                student_piece(x)
            for value in moved:
                x = x + value
        return x

    x = summed(x, ())
    (x,) = call(
        functools.partial(sweep_kernel, nb),
        [shape(nb, width)],
        [turned_crops, pltpu.VMEM((2 * rows, LANES), BF), lane_sums],
        4 * big,
        2 * big,
        0,
        x,
        own_e,
        e,
        after=(zs,),
    )
    x = summed(x, (0, 1))

    def dealt(count, many):
        height = large + count // many * 2 * padded
        return [shape(height, width)] + [shape(height, width, dtype=BF)] * (many - 1)

    scale, *x = call(
        functools.partial(last_sweep_kernel, nb, len(tots), n, rounds[0], 1 + len(rounds[1])),
        [shape(steps, 1, BLK)] + dealt(n, 1 + len(rounds[0])),
        [
            turned_crops,
            pltpu.VMEM((2 * rows, LANES), BF),
            lane_sums,
            pltpu.VMEM((large, width), F32),
            pltpu.VMEM((rows, width), F32),
        ],
        4 * big,
        2 * big,
        0,
        x,
        own_e,
        e,
        turned_ws,
        grad,
        own_tot,
        *tots,
    )
    count = n
    for k, hops in enumerate(rounds):
        pairs = [crossed(hop) if k == 1 else hop for hop in hops]
        moved = [permute(x[1 + i], "proto", pairs[i]) for i in reversed(range(len(pairs)))]
        x = [x[0]] + moved
        count //= 1 + len(hops)
        if k + 1 < len(rounds):
            x = call(
                functools.partial(deal_kernel, nb, count, rounds[k + 1]),
                dealt(count, 1 + len(rounds[k + 1])),
                [pltpu.VMEM((large, width), F32), pltpu.VMEM((count * 2 * padded, width), F32)],
                4 * count * padded * width,
                8 * count * padded * width,
                0,
                *x,
            )

    factor = protos_all * math.sqrt(width / protos_all) * (student_temp / LOG2E)
    share, lhs, ratio = call(
        functools.partial(feature_kernel, nb, len(x), factor),
        [
            shape(part, width, dtype=BF if part % 16 == 0 else F32),
            shape(here, crops, dtype=BF),
            shape(crops, LANES, dtype=BF),
        ],
        [],
        0,
        8 * rows * width,
        0,
        *x,
        student_feats,
        own_zs,
        zs,
    )

    done = ()
    for k, hops in enumerate(rounds):
        moved = permutes(share, "proto", [crossed(hop) for hop in hops])
        if k < len(weight_sizes):
            first, size = sum(weight_sizes[:k]), weight_sizes[k]
            *done, token = weight_call(
                functools.partial(
                    weight_kernel,
                    first,
                    size,
                    protos_all * math.sqrt(width / crops),
                    len(done),
                    [sum(sizes[:i]) for i in range(len(sizes) + 1)] if keep else [],
                ),
                shape(here, protos, dtype=BF),
                [
                    pltpu.VMEM((crops, BLK), BF),
                    pltpu.VMEM((size, here, BLK), BF),
                    pltpu.SemaphoreType.DMA((size,)),
                ],
                2 * big * here * size // steps,
                4 * big * size // steps,
                done,
                share,
                own_e,
                e,
                scale,
                own_zs,
                zs,
                lhs,
                ratio,
                *((own_s, *kept) if keep else (unit_ws,)),
            )
        (share,) = call(
            functools.partial(join_kernel, hops),
            [shape((1 + len(hops)) * share.shape[0], width, dtype=BF if k + 1 == len(rounds) else share.dtype)],
            [],
            0,
            8 * share.shape[0] * width,
            0,
            share,
            *moved,
            after=(token,),
        )
    return (done[0], share)


def solution(mesh):
    return jax.shard_map(
        shards,
        mesh=mesh,
        in_specs=(P("batch", None), P("batch", None), P(None, "proto"), P(None, "proto")),
        out_specs=(P("batch", "proto"), P("batch", None)),
        check_vma=False,
    )
```

```python
import functools
import math

import jax
import jax.numpy as jnp
from jax import lax
from jax.experimental import pallas as pl
from jax.experimental.pallas import tpu as pltpu
from jax.sharding import PartitionSpec as P

ITERS = 3

teacher_temp = 0.07
student_temp = 0.1
epsilon = 1e-06
LOG2E = 1.4426950408889634
BF = jnp.bfloat16
F32 = jnp.float32
MIB = 1024 * 1024
BLK = 512
LANES = 128


def dot(a, b):
    return jnp.dot(a, b, preferred_element_type=F32)


def split(values):
    high = values.astype(BF).astype(F32)
    return high, (values - high).astype(BF).astype(F32)


def split_rows(row):
    high, low = split(row)
    at = lax.broadcasted_iota(jnp.int32, (16, row.shape[1]), 0)
    return jnp.where(at == 0, high, jnp.where(at == 1, low, 0.0)).astype(BF)


def unit_rows(raw):
    values = raw.astype(F32)
    length = jnp.sqrt(jnp.sum(values * values, axis=1, keepdims=True) + epsilon)
    return values / length, length


def over(count, size, body, carry):
    if count <= 4:
        for i in range(count):
            carry = body(pl.ds(i * size, size), carry)
        return carry

    def step(i, carry):
        return body(pl.ds(pl.multiple_of(i * size, size), size), carry)

    return lax.fori_loop(0, count, step, carry)


def chunks(span):
    for at in range(0, span.size, 64):
        start = span.start + at
        yield pl.ds(start if isinstance(start, int) else pl.multiple_of(start, 64), 64)


def block(i):
    return pl.ds(pl.multiple_of(i * BLK, BLK), BLK)


def each_step(low, high, body):
    for i in range(low, high):
        body(i)


def in_turn(left, right):
    done = 0
    for k, run in enumerate(left):
        run()
        while done * len(left) < (k + 1) * len(right):
            right[done]()
            done += 1


def two_steps(steps, first, second):
    runs, result = first(0)
    in_turn(runs, [])
    for i in range(1, steps):
        carry = result()
        runs, result = first(i)
        in_turn(runs, second(i - 1, carry))
    in_turn(second(steps - 1, result()), [])


def lane_groups(values):
    out = values[:, :LANES]
    for at in range(LANES, values.shape[1], LANES):
        out = out + values[:, at : at + LANES]
    return out


def sublane_groups(values):
    return jnp.sum(values.reshape(-1, 8, values.shape[1]), axis=0)


def joined(total, nb, at=0):
    return total[at : at + nb] + total[at + nb : at + 2 * nb]


def blocks_of(crops):
    height = next(h for h in (768, 512, 256, crops) if crops % h == 0)
    return crops // height, height


def row_sums(nb, rows, acc, at=0):
    spans = [slice(at + i * rows, at + (i + 1) * rows) for i in range(nb)]
    return [jnp.sum(acc[span, :].T, axis=0, keepdims=True) for span in spans]


def put_sums(sums, out, at=0):
    for i, row in enumerate(sums):
        high, low = split(row)
        out[at + i : at + i + 1, :] = high
        out[at + len(sums) + i : at + len(sums) + i + 1, :] = low


def deal(hops, head, read, count, outs, kept, chips=0):
    many = 1 + len(hops)
    me = lax.axis_index("proto")
    digit = (me // hops[0]) % many
    for hop, out in zip((0, *hops), (kept, *outs)):
        out[0 : head.shape[0], :] = head[...].astype(out.dtype)
        for m in range(count // many):
            turn = (me // 2 % chips == m % chips).astype(jnp.int32) if chips else 0
            rows = read(m * many + (digit ^ (hop // hops[0]) ^ turn)).astype(out.dtype)
            at = head.shape[0] + m * rows.shape[0]
            out[at : at + rows.shape[0], :] = rows


def added(refs):
    acc = refs[0][...].astype(F32)
    for ref in refs[1:]:
        acc = acc + ref[...].astype(F32)
    return acc


def halves_kernel(teacher_ref, student_ref, out, sems):
    half = out.shape[0] * 2 // 3
    me = lax.axis_index("proto")
    start = pl.multiple_of(me % 2 * half, half)
    quarter = pl.multiple_of(start + me // 2 % 2 * (half // 2), half // 2)
    first = pltpu.make_async_copy(
        teacher_ref.at[pl.ds(start, half), :], out.at[0:half, :], sems.at[0]
    )
    second = pltpu.make_async_copy(
        student_ref.at[pl.ds(quarter, half // 2), :], out.at[half:, :], sems.at[1]
    )
    first.start()
    second.start()
    first.wait()
    second.wait()


def units_kernel(after, also, *refs):
    blocks, outs = refs[-3::-1], refs[-2:]
    start = 0
    for out in outs:
        size = out.shape[0] // len(blocks)
        for i, ref in enumerate(blocks):
            rows = unit_rows(ref[start : start + size, :])[0]
            out[i * size : (i + 1) * size, :] = rows.astype(BF)
        start += size


def quarters_kernel(size, after, mine, moved, out):
    side = lax.axis_index("proto") // 2 % 2
    for i in range(mine.shape[0] // size):
        for ref, place in ((mine, side), (moved, 1 - side)):
            at = pl.multiple_of((2 * i + place) * size, size)
            out[pl.ds(at, size), :] = ref[i * size : (i + 1) * size, :]


def place_kernel(mine, other, out):
    far = mine.shape[0]
    core = lax.axis_index("proto") % 2
    for ref, place in ((mine, core), (other, 1 - core)):
        out[pl.ds(pl.multiple_of(place * far, 128), far), :] = ref[...]


def weights_kernel(wt_ref, ws_ref, wt_out, ws_out, turned_out, raw, sems):
    steps = wt_out.shape[0]

    def copy(i, which):
        src = (wt_ref, ws_ref)[which]
        return pltpu.make_async_copy(src.at[:, block(i)], raw.at[which, i], sems.at[which, i])

    for which in range(2):
        for i in range(steps):
            copy(i, which).start()

    def unit(i, which):
        copy(i, which).wait()
        values = raw[which, i].astype(F32)
        length = jnp.sqrt(jnp.sum(values * values, axis=0, keepdims=True) + epsilon)
        return (values * ((LOG2E / (teacher_temp, student_temp)[which]) / length)).astype(BF)

    def teacher(i):
        wt_out[i] = unit(i, 0)

    def student(i):
        ws = unit(i, 1)
        ws_out[i] = ws
        turned_out[i] = ws.T

    each_step(0, steps, teacher)
    each_step(0, steps, student)


def add_across(rows, refs, i, ps, acc):
    own, rest = refs
    ps = ps.astype(BF)

    def add(ref, at, to):
        scaled = ref[i, at, :] * ps
        half = scaled[:, : BLK // 2] + scaled[:, BLK // 2 :]
        acc[to, :] += lane_groups(half.astype(F32))

    def many():
        def step(span, carry):
            for at in chunks(span):
                add(rest, at, pl.ds(at.start + rows, at.size))
            return carry

        over(*blocks_of(rest.shape[1]), step, 0)

    runs = [functools.partial(add, own, at, at) for at in chunks(pl.ds(0, rows))]
    if rest.shape[1] > 1024:
        return runs + [many]
    for at in chunks(pl.ds(0, rest.shape[1])):
        runs.append(functools.partial(add, rest, at, pl.ds(at.start + rows, at.size)))
    return runs


def own_first_kernel(own, wt_ref, e_ref, cols_ref, zt):
    zt[...] = unit_rows(own[...])[0].astype(BF)

    def body(i):
        e = jnp.exp2(dot(zt[...], wt_ref[i]))
        e_ref[i] = e.astype(BF)
        cols_ref[i] = sublane_groups(e)

    each_step(0, wt_ref.shape[0], body)


def exps_of(side, units, i, wt_ref, e_ref, cell):
    far = units.shape[0]
    height = 384 if far % 384 == 0 else 128
    logits = [None]

    def multiply(span):
        logits[0] = dot(units[span, :], wt_ref[i])

    def put(k, start):
        e = jnp.exp2(logits[0][k * 64 : (k + 1) * 64, :])
        e_ref[i, pl.ds(pl.multiple_of(side * far + start, 64), 64), :] = e.astype(BF)
        cell[0] = cell[0] + sublane_groups(e)

    def step(span, total):
        cell[0] = total
        multiply(span)
        for k, at in enumerate(chunks(span)):
            put(k, at.start)
        return cell[0]

    def many():
        cell[0] = over(far // height, height, step, cell[0])

    if far > height:
        return [many]
    runs = [functools.partial(multiply, pl.ds(0, far))]
    return runs + [functools.partial(put, k, k * 64) for k in range(far // 64)]


def mine_first_kernel(mine, wt_ref, own_cols, e_ref, cols_ref):
    side = lax.axis_index("proto") % 2

    def body(i):
        cell = [own_cols[i]]
        in_turn(exps_of(side, mine, i, wt_ref, e_ref, cell), [])
        cols_ref[i] = cell[0]

    each_step(0, wt_ref.shape[0], body)


def first_kernel(nb, begun, *refs):
    mine, other, wt_ref, own_ref, cols_ref, e_ref, out_ref, acc = refs[begun:]
    rows = own_ref.shape[1]
    side = lax.axis_index("proto") % 2
    acc[...] = jnp.zeros_like(acc)

    def exps(i):
        cell = [cols_ref[i]]
        runs = exps_of(1 - side, other, i, wt_ref, e_ref, cell)
        if not begun:
            runs = runs + exps_of(side, mine, i, wt_ref, e_ref, cell)
        return runs, lambda: 1.0 / jnp.sum(cell[0], axis=0, keepdims=True)

    refs = (own_ref, e_ref)
    two_steps(wt_ref.shape[0], exps, lambda i, ps: add_across(rows, refs, i, ps, acc))
    for i, row in enumerate(row_sums(nb, rows, acc)):
        out_ref[i : i + 1, :] = row


def start_sweep(nb, sums, cs, turned, acc):
    width = sums.shape[1]
    for i in range(nb):
        scale = 1.0 / sums[i : i + 1]
        span = slice(i * width, (i + 1) * width)
        if i < 2:
            turned[span, :] = jnp.broadcast_to(scale, (LANES, width)).T.astype(BF)
        else:
            cs[:, span] = split_rows(scale)
    acc[...] = jnp.zeros_like(acc)


def proto_scale(refs, i, cs, turned):
    own, rest = refs
    rows = own.shape[1]
    cell, down = [jnp.zeros((8, BLK), F32)], [None]

    def multiply():
        down[0] = dot(cs[:, 2 * rows :], rest[i, rows:, :])

    def add(ref, start, at):
        scale = turned[start + at.start : start + at.start + 64, :]
        scaled = ref[i, at, :] * jnp.concatenate([scale] * (BLK // LANES), axis=1)
        cell[0] = cell[0] + sublane_groups((scaled[:32] + scaled[32:]).astype(F32))

    runs = [multiply]
    for ref, start in ((own, 0), (rest, rows)):
        runs += [functools.partial(add, ref, start, at) for at in chunks(pl.ds(0, rows))]

    def result():
        total = jnp.sum(cell[0], axis=0, keepdims=True) + jnp.sum(down[0], axis=0, keepdims=True)
        return 1.0 / total

    return runs, result


def sweep_kernel(nb, after, x_ref, own_ref, e_ref, out_ref, cs, turned, acc):
    rows = own_ref.shape[1]
    both = (own_ref, e_ref)
    start_sweep(nb, x_ref[...], cs, turned, acc)
    two_steps(
        e_ref.shape[0],
        lambda i: proto_scale(both, i, cs, turned),
        lambda i, ps: add_across(rows, both, i, ps, acc),
    )
    for i, row in enumerate(row_sums(nb, rows, acc)):
        out_ref[i : i + 1, :] = row


def last_sweep_kernel(nb, k, n, hops, chips, x_ref, own_ref, e_ref, ws_rows, student, own_tot, *refs):
    tots, ps_ref, kept, outs = refs[:k], refs[k], refs[k + 1], refs[k + 2 : -5]
    cs, turned, acc, head, grad = refs[-5:]
    rows = own_ref.shape[1]
    both = (own_ref, e_ref)
    start_sweep(nb, x_ref[...], cs, turned, acc)
    grad[...] = jnp.zeros_like(grad)

    def across(i, ps):
        def add_grad():
            ps_ref[i] = ps
            grad[...] += dot(own_ref[i] * ps.astype(BF), ws_rows[i])

        return [add_grad] + add_across(rows, both, i, ps, acc)

    two_steps(e_ref.shape[0], lambda i: proto_scale(both, i, cs, turned), across)
    head[...] = jnp.zeros_like(head)
    put_sums(row_sums(nb, rows, acc), head)
    tot = tots[0][...]
    for more in tots[1:]:
        tot = tot + more[...]
    put_sums([own_tot[...]] + [tot[i : i + 1] for i in range(nb - 1)], head, 2 * nb)
    part = rows // n

    def read(r):
        at = pl.ds(pl.multiple_of(r * part, part), part)
        fill = [jnp.zeros((16 - part, grad.shape[1]), F32)] if part < 16 else []
        return jnp.concatenate([grad[at, :], *fill, student[at, :], *fill], axis=0)

    deal(hops, head, read, n, outs, kept, chips)


def deal_kernel(nb, count, hops, *refs):
    k = len(refs) - 3 - len(hops)
    arrived, kept, outs, (head, sums) = refs[:k], refs[k], refs[k + 1 : -2], refs[-2:]
    total = added(arrived)
    head[...] = jnp.zeros_like(head)
    for at in (0, 2 * nb):
        both = joined(total, nb, at)
        put_sums([both[i : i + 1] for i in range(nb)], head, at)
    sums[...] = total[head.shape[0] :]
    size = sums.shape[0] // count

    def read(r):
        return sums[pl.ds(pl.multiple_of(r * size, size), size), :]

    deal(hops, head, read, count, outs, kept)


def own_student_kernel(own, ws_ref, turned_ref, zs_ref, tot_ref, grad, s_ref, acc):
    zs_ref[...] = unit_rows(own[...])[0].astype(BF)
    acc[...] = jnp.zeros_like(acc)
    grad[...] = jnp.zeros_like(grad)
    kept = s_ref.shape[0] > 1

    def body(i):
        s = jnp.exp2(dot(zs_ref[...], ws_ref[i]))
        acc[...] += lane_groups(s)
        s_ref[i if kept else 0] = s.astype(BF)
        grad[...] += dot(s.astype(BF), turned_ref[i])

    each_step(0, ws_ref.shape[0], body)
    tot_ref[...] = row_sums(1, own.shape[0], acc)[0]


def student_kernel(first, count, after, zs_ref, ws_ref, tot_ref, s_ref, acc):
    acc[...] = jnp.zeros_like(acc)
    kept = s_ref.shape[0] > 1
    rows = tot_ref.shape[1]

    def body(i):
        j = i if kept else 0

        def exps(span, carry):
            logits = dot(zs_ref[span, :], ws_ref[i + first])
            for k, at in enumerate(chunks(span)):
                s = jnp.exp2(logits[k * 64 : (k + 1) * 64, :])
                acc[at, :] += lane_groups(s)
                s_ref[j, at, :] = s.astype(BF)
            return carry

        over(zs_ref.shape[0] // rows, rows, exps, 0)

    each_step(0, count, body)
    for i, row in enumerate(row_sums(tot_ref.shape[0], rows, acc)):
        tot_ref[i : i + 1, :] = row


def scaled_features(zs_refs, sums, out):
    here, width = out.shape[0], zs_refs[0].shape[1]
    at = lax.broadcasted_iota(jnp.int32, (here, width), 1)
    row = lax.broadcasted_iota(jnp.int32, (here, width), 0)
    pick = jnp.where(at == row + lax.axis_index("batch") * here, 1.0, 0.0).astype(BF)
    rows = zs_refs[0].shape[0]
    i = 0
    for ref in zs_refs:
        for start in range(0, ref.shape[0], rows):
            turned = lax.dot_general(
                pick,
                ref[start : start + rows, :],
                (((1,), (1,)), ((), ())),
                preferred_element_type=F32,
            )
            out[:, i * rows : (i + 1) * rows] = (turned * (1.0 / sums[i : i + 1])).astype(BF)
            i += 1


def feature_kernel(nb, k, factor, *refs):
    arrived, (feats_ref, own_zs, zs_ref, share_ref, lhs, ratio) = refs[:k], refs[k:]
    part, width = share_ref.shape
    rows = feats_ref.shape[0]
    padded = max(part, 16)
    total = added(arrived)
    sums, tots = joined(total, nb), joined(total, nb, 2 * nb)
    teacher, student = total[-2 * padded :][:part], total[-padded:][:part]
    at = lax.broadcasted_iota(jnp.int32, (part, rows), 1)
    row = lax.broadcasted_iota(jnp.int32, (part, rows), 0)
    pick = at == row + (lax.axis_index("proto") ^ 1) * part
    crop_scale = 1.0 / jnp.sum(jnp.where(pick, sums[0:1], 0.0), axis=1, keepdims=True)
    prob_scale = 1.0 / jnp.sum(jnp.where(pick, tots[0:1], 0.0), axis=1, keepdims=True)
    raw = dot(jnp.where(pick, 1.0, 0.0).astype(BF), feats_ref[...])
    unit, length = unit_rows(raw)
    grad = factor * (student * prob_scale - teacher * crop_scale)
    along = jnp.sum(unit * grad, axis=1, keepdims=True)
    share_ref[...] = ((grad - unit * along) / length).astype(share_ref.dtype)

    scaled_features((own_zs, zs_ref), sums, lhs)
    for i in range(nb):
        span = slice(i * rows, (i + 1) * rows)
        scale = jnp.broadcast_to(sums[i : i + 1] / tots[i : i + 1], (LANES, rows)).T
        ratio[span, :] = scale.astype(BF)


def weight_kernel(first, count, factor, aliased, starts, *refs):
    own_e, e_ref, ps_ref, own_zs, zs_ref, lhs, ratio = refs[1 + aliased : 8 + aliased]
    sources, (out_ref, token, diff, put, sems) = refs[8 + aliased : -5], refs[-5:]
    token[...] = jnp.zeros_like(token)
    rows = own_e.shape[1]

    def copy(i):
        return pltpu.make_async_copy(put.at[i], out_ref.at[:, block(i + first)], sems.at[i])

    def body(i, own_s, s_ref):
        ps = ps_ref[i].astype(BF)

        def down(zs, s, e, start):
            def step(span, acc):
                to = pl.ds(span.start + start, span.size)
                if not starts:
                    diff[to, :] = jnp.exp2(dot(zs[span, :], s[...])).astype(BF)
                for at in chunks(span):
                    to = pl.ds(at.start + start, at.size)
                    scale = jnp.concatenate([ratio[to, :]] * (BLK // LANES), axis=1)
                    left = (s[at, :] if starts else diff[to, :]) * scale
                    diff[to, :] = left - e[i, at, :] * ps
                to = pl.ds(span.start + start, span.size)
                return acc + dot(lhs[:, to], diff[to, :])

            return step

        acc = over(1, rows, down(own_zs, own_s, own_e, 0), jnp.zeros((lhs.shape[0], BLK), F32))
        acc = over(zs_ref.shape[0] // rows, rows, down(zs_ref, s_ref, e_ref, rows), acc)
        put[i - first] = (factor * acc).astype(BF)
        copy(i - first).start()

    def run(low, high, pick):
        if low < high:
            each_step(low, high, lambda i: body(i, *pick(i)))

    if starts:
        own_s, *kept = sources
        for low, high, ref in zip(starts, starts[1:], kept):
            run(
                max(low, first),
                min(high, first + count),
                lambda i, low=low, ref=ref: (own_s.at[i], ref.at[i - low]),
            )
    else:
        run(first, first + count, lambda i: (sources[0].at[i], sources[0].at[i]))
    for i in range(count):
        copy(i).wait()


def join_kernel(hops, after, share, *refs):
    moved, out_ref = refs[:-1], refs[-1]
    rows = share.shape[0]
    me = lax.axis_index("proto") ^ 1
    for hop, ref in zip((0, *hops[::-1]), (share, *moved)):
        place = ((me ^ hop) // hops[0]) % (1 + len(hops))
        out_ref[pl.ds(pl.multiple_of(place * rows, rows), rows), :] = ref[...].astype(out_ref.dtype)


def last_join_kernel(hops, after, share, *refs):
    moved, out_ref, sems = refs[:-2], refs[-2], refs[-1]
    rows = share.shape[0]
    me = lax.axis_index("proto") ^ 1
    copies = []
    for k, (hop, ref) in enumerate(zip((0, *hops[::-1]), (share, *moved))):
        place = ((me ^ hop) // hops[0]) % (1 + len(hops))
        to = out_ref.at[pl.ds(pl.multiple_of(place * rows, rows), rows), :]
        copies.append(pltpu.make_async_copy(ref, to, sems.at[k]))
    for copy in copies:
        copy.start()
    for copy in copies:
        copy.wait()


def permute(value, axis, s):
    n = lax.axis_size(axis)
    return lax.ppermute(value, axis, [(i, i ^ s) for i in range(n)])


def stages(n):
    bits = n.bit_length() - 1
    pairs = [[1 << b, 2 << b, 3 << b] if b + 1 < bits else [1 << b] for b in range(1, bits, 2)]
    return [[1]] + pairs


def permutes(value, axis, hops):
    return [permute(value, axis, hop) for hop in reversed(hops)][::-1]


def crossed(hop):
    return hop | 1


def shards(teacher_feats, student_feats, teacher_weight, student_weight):
    rows, width = teacher_feats.shape
    protos = teacher_weight.shape[1]
    nb, n = lax.axis_size("batch"), lax.axis_size("proto")
    crops, protos_all = rows * nb, protos * n
    here, part = width // nb, rows // n
    padded = max(part, 16)
    large = -(-4 * nb // 16) * 16
    keep = crops * protos <= 8 * MIB
    big = crops * protos
    wide = width * protos
    steps = protos // BLK

    limit = (16 if keep else 56) * MIB

    vmem = pl.BlockSpec(memory_space=pltpu.VMEM)
    hbm = pl.BlockSpec(memory_space=pltpu.HBM)
    anywhere = pl.BlockSpec(memory_space=pl.ANY)

    def shape(*dims, dtype=F32):
        return jax.ShapeDtypeStruct(dims, dtype)

    def call(kernel, out_shape, scratch, flops, moved, exps, *args, far=(), after=(), aliases={}):
        far = [pltpu.with_memory_space_constraint(a, pltpu.HBM) for a in far]
        return pl.pallas_call(
            kernel,
            out_shape=out_shape,
            in_specs=[hbm] * len(far)
            + [anywhere] * len(after)
            + [vmem] * len(args),
            out_specs=[vmem] * len(out_shape),
            scratch_shapes=scratch,
            input_output_aliases=aliases,
            compiler_params=pltpu.CompilerParams(vmem_limit_bytes=limit),
            cost_estimate=pl.CostEstimate(
                flops=int(flops), bytes_accessed=int(moved), transcendentals=int(exps)
            ),
        )(*far, *after, *args)

    def weight_call(kernel, out_shape, scratch, flops, moved, done, after, *args):
        return pl.pallas_call(
            kernel,
            out_shape=[out_shape, shape(8, LANES)],
            in_specs=[hbm] * len(done) + [anywhere] + [vmem] * len(args),
            out_specs=[hbm, vmem],
            scratch_shapes=scratch,
            input_output_aliases={0: 0} if done else {},
            compiler_params=pltpu.CompilerParams(vmem_limit_bytes=limit),
            cost_estimate=pl.CostEstimate(
                flops=int(flops), bytes_accessed=int(moved), transcendentals=0
            ),
        )(*done, after, *args)

    rest, half = crops - rows, rows // 2
    turned_crops = pltpu.VMEM((16, crops), BF)
    lane_sums = pltpu.VMEM((crops, LANES), F32)
    rounds = stages(n)
    sizes = [steps // 4, steps - steps // 4]
    weight_sizes = [steps // 4, steps - steps // 4]

    (mine,) = call(
        halves_kernel,
        [shape(half * 3 // 2, width, dtype=BF)],
        [pltpu.SemaphoreType.DMA((2,))],
        0,
        4 * rows * width,
        0,
        far=(teacher_feats, student_feats),
    )
    blocks = permutes(mine, "batch", range(1, nb))

    unit_wt, unit_ws, turned_ws = call(
        weights_kernel,
        [shape(steps, width, BLK, dtype=BF)] * 2 + [shape(steps, BLK, width, dtype=BF)],
        [pltpu.VMEM((2, steps, width, BLK), BF), pltpu.SemaphoreType.DMA((2, steps))],
        16 * wide,
        10 * wide,
        0,
        far=(teacher_weight, student_weight),
    )
    own_e, own_cols = call(
        own_first_kernel,
        [shape(steps, rows, BLK, dtype=BF), shape(steps, 8, BLK)],
        [pltpu.VMEM((rows, width), BF)],
        2 * rows * protos * width,
        2 * rows * protos,
        rows * protos,
        teacher_feats,
        unit_wt,
    )
    own_zs, own_tot, grad, own_s = call(
        own_student_kernel,
        [
            shape(rows, width, dtype=BF),
            shape(1, rows),
            shape(rows, width),
            shape(steps if keep else 1, rows, BLK, dtype=BF),
        ],
        [pltpu.VMEM((rows, LANES), F32)],
        4 * rows * protos * width,
        2 * rows * protos,
        rows * protos,
        student_feats,
        unit_ws,
        turned_ws,
    )

    mine, quarters = call(
        units_kernel,
        [shape(rest // 2, width, dtype=BF), shape(rest // 4, width, dtype=BF)],
        [],
        8 * crops * width,
        2 * crops * width,
        0,
        *reversed(blocks),
        after=(own_cols, own_tot),
    )
    other = permute(mine, "proto", 1)
    moved = permute(quarters, "proto", 2)

    begun, cols = (), own_cols
    if keep:
        *begun, cols = call(
            mine_first_kernel,
            [shape(steps, rest, BLK, dtype=BF), shape(steps, 8, BLK)],
            [],
            rest * protos * width,
            rest * protos,
            rest * protos // 2,
            mine,
            unit_wt,
            own_cols,
        )
    e, x = call(
        functools.partial(first_kernel, nb, len(begun)),
        [shape(steps, rest, BLK, dtype=BF), shape(nb, width)],
        [lane_sums],
        2 * big * width,
        2 * big,
        big,
        *begun,
        mine,
        other,
        unit_wt,
        own_e,
        cols,
        aliases={0: 0} if begun else {},
    )
    (student_mine,) = call(
        functools.partial(quarters_kernel, half // 2),
        [shape(rest // 2, width, dtype=BF)],
        [],
        0,
        2 * rest * width,
        0,
        quarters,
        moved,
        after=(x,),
    )
    (zs,) = call(
        place_kernel,
        [shape(rest, width, dtype=BF)],
        [],
        0,
        4 * rest * width,
        0,
        student_mine,
        permute(student_mine, "proto", 1),
    )

    tots, kept = [], []

    def student_piece(after):
        k = len(kept)
        tot, piece = call(
            functools.partial(student_kernel, sum(sizes[:k]), sizes[k]),
            [shape(nb - 1, rows), shape(sizes[k] if keep else 1, rest, BLK, dtype=BF)],
            [pltpu.VMEM((rest, LANES), F32)],
            2 * rest * width * BLK * sizes[k],
            2 * rest * BLK * sizes[k],
            rest * BLK * sizes[k],
            zs,
            unit_ws,
            after=(after,),
        )
        tots.append(tot)
        kept.append(piece)

    def summed(x, pieces):
        for k, hops in enumerate(rounds):
            moved = permutes(x, "proto", [crossed(hop) for hop in hops])
            if k in pieces:
                student_piece(x)
            for value in reversed(moved):
                x = x + value
        return x

    x = summed(x, ())
    (x,) = call(
        functools.partial(sweep_kernel, nb),
        [shape(nb, width)],
        [turned_crops, pltpu.VMEM((2 * rows, LANES), BF), lane_sums],
        4 * big,
        2 * big,
        0,
        x,
        own_e,
        e,
        after=(zs,),
    )
    x = summed(x, (0, 1))

    def dealt(count, many):
        height = large + count // many * 2 * padded
        return [shape(height, width)] + [shape(height, width, dtype=BF)] * (many - 1)

    scale, *x = call(
        functools.partial(last_sweep_kernel, nb, len(tots), n, rounds[0], 1 + len(rounds[1])),
        [shape(steps, 1, BLK)] + dealt(n, 1 + len(rounds[0])),
        [
            turned_crops,
            pltpu.VMEM((2 * rows, LANES), BF),
            lane_sums,
            pltpu.VMEM((large, width), F32),
            pltpu.VMEM((rows, width), F32),
        ],
        4 * big,
        2 * big,
        0,
        x,
        own_e,
        e,
        turned_ws,
        grad,
        own_tot,
        *tots,
    )
    count = n
    for k, hops in enumerate(rounds):
        pairs = [crossed(hop) if k == 1 else hop for hop in hops]
        moved = [permute(x[1 + i], "proto", pairs[i]) for i in reversed(range(len(pairs)))]
        x = [x[0]] + moved
        count //= 1 + len(hops)
        if k + 1 < len(rounds):
            x = call(
                functools.partial(deal_kernel, nb, count, rounds[k + 1]),
                dealt(count, 1 + len(rounds[k + 1])),
                [pltpu.VMEM((large, width), F32), pltpu.VMEM((count * 2 * padded, width), F32)],
                4 * count * padded * width,
                8 * count * padded * width,
                0,
                *x,
            )

    factor = protos_all * math.sqrt(width / protos_all) * (student_temp / LOG2E)
    share, lhs, ratio = call(
        functools.partial(feature_kernel, nb, len(x), factor),
        [
            shape(part, width, dtype=BF if part % 16 == 0 else F32),
            shape(here, crops, dtype=BF),
            shape(crops, LANES, dtype=BF),
        ],
        [],
        0,
        8 * rows * width,
        0,
        *x,
        student_feats,
        own_zs,
        zs,
    )

    done = ()
    for k, hops in enumerate(rounds):
        moved = permutes(share, "proto", [crossed(hop) for hop in hops])
        if k < len(weight_sizes):
            first, size = sum(weight_sizes[:k]), weight_sizes[k]
            *done, token = weight_call(
                functools.partial(
                    weight_kernel,
                    first,
                    size,
                    protos_all * math.sqrt(width / crops),
                    len(done),
                    [sum(sizes[:i]) for i in range(len(sizes) + 1)] if keep else [],
                ),
                shape(here, protos, dtype=BF),
                [
                    pltpu.VMEM((crops, BLK), BF),
                    pltpu.VMEM((size, here, BLK), BF),
                    pltpu.SemaphoreType.DMA((size,)),
                ],
                2 * big * here * size // steps,
                4 * big * size // steps,
                done,
                share,
                own_e,
                e,
                scale,
                own_zs,
                zs,
                lhs,
                ratio,
                *((own_s, *kept) if keep else (unit_ws,)),
            )
        if k + 1 == len(rounds) and share.dtype == BF:
            (share,) = pl.pallas_call(
                functools.partial(last_join_kernel, hops),
                out_shape=[shape(rows, width, dtype=BF)],
                in_specs=[anywhere] + [vmem] * (1 + len(moved)),
                out_specs=[hbm],
                scratch_shapes=[pltpu.SemaphoreType.DMA((1 + len(moved),))],
                compiler_params=pltpu.CompilerParams(vmem_limit_bytes=limit),
            )(token, share, *reversed(moved))
            break
        (share,) = call(
            functools.partial(join_kernel, hops),
            [shape((1 + len(hops)) * share.shape[0], width, dtype=BF if k + 1 == len(rounds) else share.dtype)],
            [],
            0,
            8 * share.shape[0] * width,
            0,
            share,
            *reversed(moved),
            after=(token,),
        )
    return (done[0], share)


def solution(mesh):
    return jax.shard_map(
        shards,
        mesh=mesh,
        in_specs=(P("batch", None), P("batch", None), P(None, "proto"), P(None, "proto")),
        out_specs=(P("batch", "proto"), P("batch", None)),
        check_vma=False,
    )
```

```python
import functools
import math

import jax
import jax.numpy as jnp
from jax import lax
from jax.experimental import pallas as pl
from jax.experimental.pallas import tpu as pltpu
from jax.sharding import PartitionSpec as P

ITERS = 3

teacher_temp = 0.07
student_temp = 0.1
epsilon = 1e-06
LOG2E = 1.4426950408889634
BF = jnp.bfloat16
F32 = jnp.float32
MIB = 1024 * 1024
BLK = 512
LANES = 128


def dot(a, b):
    return jnp.dot(a, b, preferred_element_type=F32)


def split(values):
    high = values.astype(BF).astype(F32)
    return high, (values - high).astype(BF).astype(F32)


def split_rows(row):
    high, low = split(row)
    at = lax.broadcasted_iota(jnp.int32, (16, row.shape[1]), 0)
    return jnp.where(at == 0, high, jnp.where(at == 1, low, 0.0)).astype(BF)


def unit_rows(raw):
    values = raw.astype(F32)
    length = jnp.sqrt(jnp.sum(values * values, axis=1, keepdims=True) + epsilon)
    return values / length, length


def over(count, size, body, carry):
    if count <= 4:
        for i in range(count):
            carry = body(pl.ds(i * size, size), carry)
        return carry

    def step(i, carry):
        return body(pl.ds(pl.multiple_of(i * size, size), size), carry)

    return lax.fori_loop(0, count, step, carry)


def chunks(span):
    for at in range(0, span.size, 64):
        start = span.start + at
        yield pl.ds(start if isinstance(start, int) else pl.multiple_of(start, 64), 64)


def block(i):
    return pl.ds(pl.multiple_of(i * BLK, BLK), BLK)


def each_step(low, high, body):
    for i in range(low, high):
        body(i)


def in_turn(left, right):
    done = 0
    for k, run in enumerate(left):
        run()
        while done * len(left) < (k + 1) * len(right):
            right[done]()
            done += 1


def two_steps(steps, first, second):
    runs, result = first(0)
    in_turn(runs, [])
    for i in range(1, steps):
        carry = result()
        runs, result = first(i)
        in_turn(runs, second(i - 1, carry))
    in_turn(second(steps - 1, result()), [])


def lane_groups(values):
    out = values[:, :LANES]
    for at in range(LANES, values.shape[1], LANES):
        out = out + values[:, at : at + LANES]
    return out


def sublane_groups(values):
    return jnp.sum(values.reshape(-1, 8, values.shape[1]), axis=0)


def joined(total, nb, at=0):
    return total[at : at + nb] + total[at + nb : at + 2 * nb]


def blocks_of(crops):
    height = next(h for h in (768, 512, 256, crops) if crops % h == 0)
    return crops // height, height


def row_sums(nb, rows, acc, at=0):
    spans = [slice(at + i * rows, at + (i + 1) * rows) for i in range(nb)]
    return [jnp.sum(acc[span, :].T, axis=0, keepdims=True) for span in spans]


def put_sums(sums, out, at=0):
    for i, row in enumerate(sums):
        high, low = split(row)
        out[at + i : at + i + 1, :] = high
        out[at + len(sums) + i : at + len(sums) + i + 1, :] = low


def deal(hops, head, read, count, outs, kept, chips=0):
    many = 1 + len(hops)
    me = lax.axis_index("proto")
    digit = (me // hops[0]) % many
    for hop, out in zip((0, *hops), (kept, *outs)):
        out[0 : head.shape[0], :] = head[...].astype(out.dtype)
        for m in range(count // many):
            turn = (me // 2 % chips == m % chips).astype(jnp.int32) if chips else 0
            rows = read(m * many + (digit ^ (hop // hops[0]) ^ turn)).astype(out.dtype)
            at = head.shape[0] + m * rows.shape[0]
            out[at : at + rows.shape[0], :] = rows


def added(refs):
    acc = refs[0][...].astype(F32)
    for ref in refs[1:]:
        acc = acc + ref[...].astype(F32)
    return acc


def halves_kernel(teacher_ref, student_ref, out, sems):
    half = out.shape[0] * 2 // 3
    me = lax.axis_index("proto")
    start = pl.multiple_of(me % 2 * half, half)
    quarter = pl.multiple_of(start + me // 2 % 2 * (half // 2), half // 2)
    first = pltpu.make_async_copy(
        teacher_ref.at[pl.ds(start, half), :], out.at[0:half, :], sems.at[0]
    )
    second = pltpu.make_async_copy(
        student_ref.at[pl.ds(quarter, half // 2), :], out.at[half:, :], sems.at[1]
    )
    first.start()
    second.start()
    first.wait()
    second.wait()


def units_kernel(after, also, *refs):
    blocks, outs = refs[-3::-1], refs[-2:]
    start = 0
    for out in outs:
        size = out.shape[0] // len(blocks)
        for i, ref in enumerate(blocks):
            rows = unit_rows(ref[start : start + size, :])[0]
            out[i * size : (i + 1) * size, :] = rows.astype(BF)
        start += size


def quarters_kernel(after, mine, moved, out):
    size = mine.shape[0]
    out[0:size, :] = mine[...]
    out[size:, :] = moved[...]


def place_kernel(size, mine, other, out):
    far = mine.shape[0]
    me = lax.axis_index("proto")
    core, side = me % 2, me // 2 % 2
    for ref, own in ((mine, core), (other, 1 - core)):
        for k, (half, quarter) in enumerate(((own, side), (1 - own, 1 - side))):
            for i in range(far // (2 * size)):
                at = pl.multiple_of(half * far + (2 * i + quarter) * size, size)
                start = k * (far // 2) + i * size
                out[pl.ds(at, size), :] = ref[start : start + size, :]


def weights_kernel(wt_ref, ws_ref, wt_out, ws_out, turned_out, raw, sems):
    steps = wt_out.shape[0]

    def copy(i, which):
        src = (wt_ref, ws_ref)[which]
        return pltpu.make_async_copy(src.at[:, block(i)], raw.at[which, i], sems.at[which, i])

    for which in range(2):
        for i in range(steps):
            copy(i, which).start()

    def unit(i, which):
        copy(i, which).wait()
        values = raw[which, i].astype(F32)
        length = jnp.sqrt(jnp.sum(values * values, axis=0, keepdims=True) + epsilon)
        return (values * ((LOG2E / (teacher_temp, student_temp)[which]) / length)).astype(BF)

    def teacher(i):
        wt_out[i] = unit(i, 0)

    def student(i):
        ws = unit(i, 1)
        ws_out[i] = ws
        turned_out[i] = ws.T

    each_step(0, steps, teacher)
    each_step(0, steps, student)


def add_across(rows, refs, i, ps, acc):
    own, rest = refs
    ps = ps.astype(BF)

    def add(ref, at, to):
        scaled = ref[i, at, :] * ps
        half = scaled[:, : BLK // 2] + scaled[:, BLK // 2 :]
        acc[to, :] += lane_groups(half.astype(F32))

    def many():
        def step(span, carry):
            for at in chunks(span):
                add(rest, at, pl.ds(at.start + rows, at.size))
            return carry

        over(*blocks_of(rest.shape[1]), step, 0)

    runs = [functools.partial(add, own, at, at) for at in chunks(pl.ds(0, rows))]
    if rest.shape[1] > 1024:
        return runs + [many]
    for at in chunks(pl.ds(0, rest.shape[1])):
        runs.append(functools.partial(add, rest, at, pl.ds(at.start + rows, at.size)))
    return runs


def own_first_kernel(own, wt_ref, e_ref, cols_ref, zt):
    zt[...] = unit_rows(own[...])[0].astype(BF)

    def body(i):
        e = jnp.exp2(dot(zt[...], wt_ref[i]))
        e_ref[i] = e.astype(BF)
        cols_ref[i] = sublane_groups(e)

    each_step(0, wt_ref.shape[0], body)


def exps_of(side, units, i, wt_ref, e_ref, cell):
    far = units.shape[0]
    height = 384 if far % 384 == 0 else 128
    logits = [None]

    def multiply(span):
        logits[0] = dot(units[span, :], wt_ref[i])

    def put(k, start):
        e = jnp.exp2(logits[0][k * 64 : (k + 1) * 64, :])
        e_ref[i, pl.ds(pl.multiple_of(side * far + start, 64), 64), :] = e.astype(BF)
        cell[0] = cell[0] + sublane_groups(e)

    def step(span, total):
        cell[0] = total
        multiply(span)
        for k, at in enumerate(chunks(span)):
            put(k, at.start)
        return cell[0]

    def many():
        cell[0] = over(far // height, height, step, cell[0])

    if far > height:
        return [many]
    runs = [functools.partial(multiply, pl.ds(0, far))]
    return runs + [functools.partial(put, k, k * 64) for k in range(far // 64)]


def mine_first_kernel(mine, wt_ref, own_cols, e_ref, cols_ref):
    side = lax.axis_index("proto") % 2

    def body(i):
        cell = [own_cols[i]]
        in_turn(exps_of(side, mine, i, wt_ref, e_ref, cell), [])
        cols_ref[i] = cell[0]

    each_step(0, wt_ref.shape[0], body)


def first_kernel(nb, begun, *refs):
    mine, other, wt_ref, own_ref, cols_ref, e_ref, out_ref, acc = refs[begun:]
    rows = own_ref.shape[1]
    side = lax.axis_index("proto") % 2
    acc[...] = jnp.zeros_like(acc)

    def exps(i):
        cell = [cols_ref[i]]
        runs = exps_of(1 - side, other, i, wt_ref, e_ref, cell)
        if not begun:
            runs = runs + exps_of(side, mine, i, wt_ref, e_ref, cell)
        return runs, lambda: 1.0 / jnp.sum(cell[0], axis=0, keepdims=True)

    refs = (own_ref, e_ref)
    two_steps(wt_ref.shape[0], exps, lambda i, ps: add_across(rows, refs, i, ps, acc))
    for i, row in enumerate(row_sums(nb, rows, acc)):
        out_ref[i : i + 1, :] = row


def start_sweep(nb, sums, cs, turned, acc):
    width = sums.shape[1]
    for i in range(nb):
        scale = 1.0 / sums[i : i + 1]
        span = slice(i * width, (i + 1) * width)
        if i < 2:
            turned[span, :] = jnp.broadcast_to(scale, (LANES, width)).T.astype(BF)
        else:
            cs[:, span] = split_rows(scale)
    acc[...] = jnp.zeros_like(acc)


def proto_scale(refs, i, cs, turned):
    own, rest = refs
    rows = own.shape[1]
    cell, down = [jnp.zeros((8, BLK), F32)], [None]

    def multiply():
        down[0] = dot(cs[:, 2 * rows :], rest[i, rows:, :])

    def add(ref, start, at):
        scale = turned[start + at.start : start + at.start + 64, :]
        scaled = ref[i, at, :] * jnp.concatenate([scale] * (BLK // LANES), axis=1)
        cell[0] = cell[0] + sublane_groups((scaled[:32] + scaled[32:]).astype(F32))

    runs = [multiply]
    for ref, start in ((own, 0), (rest, rows)):
        runs += [functools.partial(add, ref, start, at) for at in chunks(pl.ds(0, rows))]

    def result():
        total = jnp.sum(cell[0], axis=0, keepdims=True) + jnp.sum(down[0], axis=0, keepdims=True)
        return 1.0 / total

    return runs, result


def sweep_kernel(nb, after, x_ref, own_ref, e_ref, out_ref, cs, turned, acc):
    rows = own_ref.shape[1]
    both = (own_ref, e_ref)
    start_sweep(nb, x_ref[...], cs, turned, acc)
    two_steps(
        e_ref.shape[0],
        lambda i: proto_scale(both, i, cs, turned),
        lambda i, ps: add_across(rows, both, i, ps, acc),
    )
    for i, row in enumerate(row_sums(nb, rows, acc)):
        out_ref[i : i + 1, :] = row


def last_sweep_kernel(nb, k, n, hops, chips, x_ref, own_ref, e_ref, ws_rows, student, own_tot, *refs):
    tots, ps_ref, kept, outs = refs[:k], refs[k], refs[k + 1], refs[k + 2 : -5]
    cs, turned, acc, head, grad = refs[-5:]
    rows = own_ref.shape[1]
    both = (own_ref, e_ref)
    start_sweep(nb, x_ref[...], cs, turned, acc)
    grad[...] = jnp.zeros_like(grad)

    def across(i, ps):
        def add_grad():
            ps_ref[i] = ps
            grad[...] += dot(own_ref[i] * ps.astype(BF), ws_rows[i])

        return [add_grad] + add_across(rows, both, i, ps, acc)

    two_steps(e_ref.shape[0], lambda i: proto_scale(both, i, cs, turned), across)
    head[...] = jnp.zeros_like(head)
    put_sums(row_sums(nb, rows, acc), head)
    tot = tots[0][...]
    for more in tots[1:]:
        tot = tot + more[...]
    put_sums([own_tot[...]] + [tot[i : i + 1] for i in range(nb - 1)], head, 2 * nb)
    part = rows // n

    def read(r):
        at = pl.ds(pl.multiple_of(r * part, part), part)
        fill = [jnp.zeros((16 - part, grad.shape[1]), F32)] if part < 16 else []
        return jnp.concatenate([grad[at, :], *fill, student[at, :], *fill], axis=0)

    deal(hops, head, read, n, outs, kept, chips)


def deal_kernel(nb, count, hops, *refs):
    k = len(refs) - 3 - len(hops)
    arrived, kept, outs, (head, sums) = refs[:k], refs[k], refs[k + 1 : -2], refs[-2:]
    total = added(arrived)
    head[...] = jnp.zeros_like(head)
    for at in (0, 2 * nb):
        both = joined(total, nb, at)
        put_sums([both[i : i + 1] for i in range(nb)], head, at)
    sums[...] = total[head.shape[0] :]
    size = sums.shape[0] // count

    def read(r):
        return sums[pl.ds(pl.multiple_of(r * size, size), size), :]

    deal(hops, head, read, count, outs, kept)


def own_student_kernel(own, ws_ref, turned_ref, zs_ref, tot_ref, grad, s_ref, acc):
    zs_ref[...] = unit_rows(own[...])[0].astype(BF)
    acc[...] = jnp.zeros_like(acc)
    grad[...] = jnp.zeros_like(grad)
    kept = s_ref.shape[0] > 1

    def body(i):
        s = jnp.exp2(dot(zs_ref[...], ws_ref[i]))
        acc[...] += lane_groups(s)
        s_ref[i if kept else 0] = s.astype(BF)
        grad[...] += dot(s.astype(BF), turned_ref[i])

    each_step(0, ws_ref.shape[0], body)
    tot_ref[...] = row_sums(1, own.shape[0], acc)[0]


def student_kernel(first, count, after, zs_ref, ws_ref, tot_ref, s_ref, acc):
    acc[...] = jnp.zeros_like(acc)
    kept = s_ref.shape[0] > 1
    rows = tot_ref.shape[1]

    def body(i):
        j = i if kept else 0

        def exps(span, carry):
            logits = dot(zs_ref[span, :], ws_ref[i + first])
            for k, at in enumerate(chunks(span)):
                s = jnp.exp2(logits[k * 64 : (k + 1) * 64, :])
                acc[at, :] += lane_groups(s)
                s_ref[j, at, :] = s.astype(BF)
            return carry

        over(zs_ref.shape[0] // rows, rows, exps, 0)

    each_step(0, count, body)
    for i, row in enumerate(row_sums(tot_ref.shape[0], rows, acc)):
        tot_ref[i : i + 1, :] = row


def scaled_features(zs_refs, sums, out):
    here, width = out.shape[0], zs_refs[0].shape[1]
    at = lax.broadcasted_iota(jnp.int32, (here, width), 1)
    row = lax.broadcasted_iota(jnp.int32, (here, width), 0)
    pick = jnp.where(at == row + lax.axis_index("batch") * here, 1.0, 0.0).astype(BF)
    rows = zs_refs[0].shape[0]
    i = 0
    for ref in zs_refs:
        for start in range(0, ref.shape[0], rows):
            turned = lax.dot_general(
                pick,
                ref[start : start + rows, :],
                (((1,), (1,)), ((), ())),
                preferred_element_type=F32,
            )
            out[:, i * rows : (i + 1) * rows] = (turned * (1.0 / sums[i : i + 1])).astype(BF)
            i += 1


def feature_kernel(nb, k, factor, *refs):
    arrived, (feats_ref, own_zs, zs_ref, share_ref, lhs, ratio) = refs[:k], refs[k:]
    part, width = share_ref.shape
    rows = feats_ref.shape[0]
    padded = max(part, 16)
    total = added(arrived)
    sums, tots = joined(total, nb), joined(total, nb, 2 * nb)
    teacher, student = total[-2 * padded :][:part], total[-padded:][:part]
    at = lax.broadcasted_iota(jnp.int32, (part, rows), 1)
    row = lax.broadcasted_iota(jnp.int32, (part, rows), 0)
    pick = at == row + (lax.axis_index("proto") ^ 1) * part
    crop_scale = 1.0 / jnp.sum(jnp.where(pick, sums[0:1], 0.0), axis=1, keepdims=True)
    prob_scale = 1.0 / jnp.sum(jnp.where(pick, tots[0:1], 0.0), axis=1, keepdims=True)
    raw = dot(jnp.where(pick, 1.0, 0.0).astype(BF), feats_ref[...])
    unit, length = unit_rows(raw)
    grad = factor * (student * prob_scale - teacher * crop_scale)
    along = jnp.sum(unit * grad, axis=1, keepdims=True)
    share_ref[...] = ((grad - unit * along) / length).astype(share_ref.dtype)

    scaled_features((own_zs, zs_ref), sums, lhs)
    for i in range(nb):
        span = slice(i * rows, (i + 1) * rows)
        scale = jnp.broadcast_to(sums[i : i + 1] / tots[i : i + 1], (LANES, rows)).T
        ratio[span, :] = scale.astype(BF)


def weight_kernel(first, count, factor, aliased, starts, *refs):
    own_e, e_ref, ps_ref, own_zs, zs_ref, lhs, ratio = refs[1 + aliased : 8 + aliased]
    sources, (out_ref, token, diff, put, sems) = refs[8 + aliased : -5], refs[-5:]
    token[...] = jnp.zeros_like(token)
    rows = own_e.shape[1]

    def copy(i):
        return pltpu.make_async_copy(put.at[i], out_ref.at[:, block(i + first)], sems.at[i])

    def body(i, own_s, s_ref):
        ps = ps_ref[i].astype(BF)

        def down(zs, s, e, start):
            def step(span, acc):
                to = pl.ds(span.start + start, span.size)
                if not starts:
                    diff[to, :] = jnp.exp2(dot(zs[span, :], s[...])).astype(BF)
                for at in chunks(span):
                    to = pl.ds(at.start + start, at.size)
                    scale = jnp.concatenate([ratio[to, :]] * (BLK // LANES), axis=1)
                    left = (s[at, :] if starts else diff[to, :]) * scale
                    diff[to, :] = left - e[i, at, :] * ps
                to = pl.ds(span.start + start, span.size)
                return acc + dot(lhs[:, to], diff[to, :])

            return step

        acc = over(1, rows, down(own_zs, own_s, own_e, 0), jnp.zeros((lhs.shape[0], BLK), F32))
        acc = over(zs_ref.shape[0] // rows, rows, down(zs_ref, s_ref, e_ref, rows), acc)
        put[i - first] = (factor * acc).astype(BF)
        copy(i - first).start()

    def run(low, high, pick):
        if low < high:
            each_step(low, high, lambda i: body(i, *pick(i)))

    if starts:
        own_s, *kept = sources
        for low, high, ref in zip(starts, starts[1:], kept):
            run(
                max(low, first),
                min(high, first + count),
                lambda i, low=low, ref=ref: (own_s.at[i], ref.at[i - low]),
            )
    else:
        run(first, first + count, lambda i: (sources[0].at[i], sources[0].at[i]))
    for i in range(count):
        copy(i).wait()


def join_kernel(hops, after, share, *refs):
    moved, out_ref = refs[:-1], refs[-1]
    rows = share.shape[0]
    me = lax.axis_index("proto") ^ 1
    for hop, ref in zip((0, *hops[::-1]), (share, *moved)):
        place = ((me ^ hop) // hops[0]) % (1 + len(hops))
        out_ref[pl.ds(pl.multiple_of(place * rows, rows), rows), :] = ref[...].astype(out_ref.dtype)


def last_join_kernel(hops, after, share, *refs):
    moved, out_ref, sems = refs[:-2], refs[-2], refs[-1]
    rows = share.shape[0]
    me = lax.axis_index("proto") ^ 1
    copies = []
    for k, (hop, ref) in enumerate(zip((0, *hops[::-1]), (share, *moved))):
        place = ((me ^ hop) // hops[0]) % (1 + len(hops))
        to = out_ref.at[pl.ds(pl.multiple_of(place * rows, rows), rows), :]
        copies.append(pltpu.make_async_copy(ref, to, sems.at[k]))
    for copy in copies:
        copy.start()
    for copy in copies:
        copy.wait()


def permute(value, axis, s):
    n = lax.axis_size(axis)
    return lax.ppermute(value, axis, [(i, i ^ s) for i in range(n)])


def stages(n):
    bits = n.bit_length() - 1
    pairs = [[1 << b, 2 << b, 3 << b] if b + 1 < bits else [1 << b] for b in range(1, bits, 2)]
    return [[1]] + pairs


def permutes(value, axis, hops):
    return [permute(value, axis, hop) for hop in reversed(hops)][::-1]


def crossed(hop):
    return hop | 1


def shards(teacher_feats, student_feats, teacher_weight, student_weight):
    rows, width = teacher_feats.shape
    protos = teacher_weight.shape[1]
    nb, n = lax.axis_size("batch"), lax.axis_size("proto")
    crops, protos_all = rows * nb, protos * n
    here, part = width // nb, rows // n
    padded = max(part, 16)
    large = -(-4 * nb // 16) * 16
    keep = crops * protos <= 8 * MIB
    big = crops * protos
    wide = width * protos
    steps = protos // BLK

    limit = (16 if keep else 56) * MIB

    vmem = pl.BlockSpec(memory_space=pltpu.VMEM)
    hbm = pl.BlockSpec(memory_space=pltpu.HBM)
    anywhere = pl.BlockSpec(memory_space=pl.ANY)

    def shape(*dims, dtype=F32):
        return jax.ShapeDtypeStruct(dims, dtype)

    def call(kernel, out_shape, scratch, flops, moved, exps, *args, far=(), after=(), aliases={}):
        far = [pltpu.with_memory_space_constraint(a, pltpu.HBM) for a in far]
        return pl.pallas_call(
            kernel,
            out_shape=out_shape,
            in_specs=[hbm] * len(far)
            + [anywhere] * len(after)
            + [vmem] * len(args),
            out_specs=[vmem] * len(out_shape),
            scratch_shapes=scratch,
            input_output_aliases=aliases,
            compiler_params=pltpu.CompilerParams(vmem_limit_bytes=limit),
            cost_estimate=pl.CostEstimate(
                flops=int(flops), bytes_accessed=int(moved), transcendentals=int(exps)
            ),
        )(*far, *after, *args)

    def weight_call(kernel, out_shape, scratch, flops, moved, done, after, *args):
        return pl.pallas_call(
            kernel,
            out_shape=[out_shape, shape(8, LANES)],
            in_specs=[hbm] * len(done) + [anywhere] + [vmem] * len(args),
            out_specs=[hbm, vmem],
            scratch_shapes=scratch,
            input_output_aliases={0: 0} if done else {},
            compiler_params=pltpu.CompilerParams(vmem_limit_bytes=limit),
            cost_estimate=pl.CostEstimate(
                flops=int(flops), bytes_accessed=int(moved), transcendentals=0
            ),
        )(*done, after, *args)

    rest, half = crops - rows, rows // 2
    turned_crops = pltpu.VMEM((16, crops), BF)
    lane_sums = pltpu.VMEM((crops, LANES), F32)
    rounds = stages(n)
    sizes = [steps // 4, steps - steps // 4]
    weight_sizes = [steps // 8, steps - steps // 8]

    (mine,) = call(
        halves_kernel,
        [shape(half * 3 // 2, width, dtype=BF)],
        [pltpu.SemaphoreType.DMA((2,))],
        0,
        4 * rows * width,
        0,
        far=(teacher_feats, student_feats),
    )
    blocks = permutes(mine, "batch", range(1, nb))

    unit_wt, unit_ws, turned_ws = call(
        weights_kernel,
        [shape(steps, width, BLK, dtype=BF)] * 2 + [shape(steps, BLK, width, dtype=BF)],
        [pltpu.VMEM((2, steps, width, BLK), BF), pltpu.SemaphoreType.DMA((2, steps))],
        16 * wide,
        10 * wide,
        0,
        far=(teacher_weight, student_weight),
    )
    own_e, own_cols = call(
        own_first_kernel,
        [shape(steps, rows, BLK, dtype=BF), shape(steps, 8, BLK)],
        [pltpu.VMEM((rows, width), BF)],
        2 * rows * protos * width,
        2 * rows * protos,
        rows * protos,
        teacher_feats,
        unit_wt,
    )
    own_zs, own_tot, grad, own_s = call(
        own_student_kernel,
        [
            shape(rows, width, dtype=BF),
            shape(1, rows),
            shape(rows, width),
            shape(steps if keep else 1, rows, BLK, dtype=BF),
        ],
        [pltpu.VMEM((rows, LANES), F32)],
        4 * rows * protos * width,
        2 * rows * protos,
        rows * protos,
        student_feats,
        unit_ws,
        turned_ws,
    )

    mine, quarters = call(
        units_kernel,
        [shape(rest // 2, width, dtype=BF), shape(rest // 4, width, dtype=BF)],
        [],
        8 * crops * width,
        2 * crops * width,
        0,
        *reversed(blocks),
        after=(own_cols, own_tot),
    )
    other = permute(mine, "proto", 1)
    moved = permute(quarters, "proto", crossed(2))

    begun, cols = (), own_cols
    if keep:
        *begun, cols = call(
            mine_first_kernel,
            [shape(steps, rest, BLK, dtype=BF), shape(steps, 8, BLK)],
            [],
            rest * protos * width,
            rest * protos,
            rest * protos // 2,
            mine,
            unit_wt,
            own_cols,
        )
    e, x = call(
        functools.partial(first_kernel, nb, len(begun)),
        [shape(steps, rest, BLK, dtype=BF), shape(nb, width)],
        [lane_sums],
        2 * big * width,
        2 * big,
        big,
        *begun,
        mine,
        other,
        unit_wt,
        own_e,
        cols,
        aliases={0: 0} if begun else {},
    )
    (student_mine,) = call(
        quarters_kernel,
        [shape(rest // 2, width, dtype=BF)],
        [],
        0,
        2 * rest * width,
        0,
        quarters,
        moved,
        after=(x,),
    )
    (zs,) = call(
        functools.partial(place_kernel, half // 2),
        [shape(rest, width, dtype=BF)],
        [],
        0,
        4 * rest * width,
        0,
        student_mine,
        permute(student_mine, "proto", 1),
    )

    tots, kept = [], []

    def student_piece(after):
        k = len(kept)
        tot, piece = call(
            functools.partial(student_kernel, sum(sizes[:k]), sizes[k]),
            [shape(nb - 1, rows), shape(sizes[k] if keep else 1, rest, BLK, dtype=BF)],
            [pltpu.VMEM((rest, LANES), F32)],
            2 * rest * width * BLK * sizes[k],
            2 * rest * BLK * sizes[k],
            rest * BLK * sizes[k],
            zs,
            unit_ws,
            after=(after,),
        )
        tots.append(tot)
        kept.append(piece)

    def summed(x, pieces):
        for k, hops in enumerate(rounds):
            moved = permutes(x, "proto", [crossed(hop) for hop in hops])
            if k in pieces:
                student_piece(x)
            for value in reversed(moved):
                x = x + value
        return x

    x = summed(x, ())
    (x,) = call(
        functools.partial(sweep_kernel, nb),
        [shape(nb, width)],
        [turned_crops, pltpu.VMEM((2 * rows, LANES), BF), lane_sums],
        4 * big,
        2 * big,
        0,
        x,
        own_e,
        e,
        after=(zs,),
    )
    x = summed(x, (0, 1))

    def dealt(count, many):
        height = large + count // many * 2 * padded
        return [shape(height, width)] + [shape(height, width, dtype=BF)] * (many - 1)

    scale, *x = call(
        functools.partial(last_sweep_kernel, nb, len(tots), n, rounds[0], 1 + len(rounds[1])),
        [shape(steps, 1, BLK)] + dealt(n, 1 + len(rounds[0])),
        [
            turned_crops,
            pltpu.VMEM((2 * rows, LANES), BF),
            lane_sums,
            pltpu.VMEM((large, width), F32),
            pltpu.VMEM((rows, width), F32),
        ],
        4 * big,
        2 * big,
        0,
        x,
        own_e,
        e,
        turned_ws,
        grad,
        own_tot,
        *tots,
    )
    count = n
    for k, hops in enumerate(rounds):
        pairs = [crossed(hop) if k == 1 else hop for hop in hops]
        moved = [permute(x[1 + i], "proto", pairs[i]) for i in reversed(range(len(pairs)))]
        x = [x[0]] + moved
        count //= 1 + len(hops)
        if k + 1 < len(rounds):
            x = call(
                functools.partial(deal_kernel, nb, count, rounds[k + 1]),
                dealt(count, 1 + len(rounds[k + 1])),
                [pltpu.VMEM((large, width), F32), pltpu.VMEM((count * 2 * padded, width), F32)],
                4 * count * padded * width,
                8 * count * padded * width,
                0,
                *x,
            )

    factor = protos_all * math.sqrt(width / protos_all) * (student_temp / LOG2E)
    share, lhs, ratio = call(
        functools.partial(feature_kernel, nb, len(x), factor),
        [
            shape(part, width, dtype=BF if part % 16 == 0 else F32),
            shape(here, crops, dtype=BF),
            shape(crops, LANES, dtype=BF),
        ],
        [],
        0,
        8 * rows * width,
        0,
        *x,
        student_feats,
        own_zs,
        zs,
    )

    done = ()
    for k, hops in enumerate(rounds):
        moved = permutes(share, "proto", [crossed(hop) for hop in hops])
        if k < len(weight_sizes):
            first, size = sum(weight_sizes[:k]), weight_sizes[k]
            *done, token = weight_call(
                functools.partial(
                    weight_kernel,
                    first,
                    size,
                    protos_all * math.sqrt(width / crops),
                    len(done),
                    [sum(sizes[:i]) for i in range(len(sizes) + 1)] if keep else [],
                ),
                shape(here, protos, dtype=BF),
                [
                    pltpu.VMEM((crops, BLK), BF),
                    pltpu.VMEM((size, here, BLK), BF),
                    pltpu.SemaphoreType.DMA((size,)),
                ],
                2 * big * here * size // steps,
                4 * big * size // steps,
                done,
                share,
                own_e,
                e,
                scale,
                own_zs,
                zs,
                lhs,
                ratio,
                *((own_s, *kept) if keep else (unit_ws,)),
            )
        if k + 1 == len(rounds) and share.dtype == BF:
            (share,) = pl.pallas_call(
                functools.partial(last_join_kernel, hops),
                out_shape=[shape(rows, width, dtype=BF)],
                in_specs=[anywhere] + [vmem] * (1 + len(moved)),
                out_specs=[hbm],
                scratch_shapes=[pltpu.SemaphoreType.DMA((1 + len(moved),))],
                compiler_params=pltpu.CompilerParams(vmem_limit_bytes=limit),
            )(token, share, *reversed(moved))
            break
        (share,) = call(
            functools.partial(join_kernel, hops),
            [shape((1 + len(hops)) * share.shape[0], width, dtype=BF if k + 1 == len(rounds) else share.dtype)],
            [],
            0,
            8 * share.shape[0] * width,
            0,
            share,
            *reversed(moved),
            after=(token,),
        )
    return (done[0], share)


def solution(mesh):
    return jax.shard_map(
        shards,
        mesh=mesh,
        in_specs=(P("batch", None), P("batch", None), P(None, "proto"), P(None, "proto")),
        out_specs=(P("batch", "proto"), P("batch", None)),
        check_vma=False,
    )
```

```python
import functools
import math

import jax
import jax.numpy as jnp
from jax import lax
from jax.experimental import pallas as pl
from jax.experimental.pallas import tpu as pltpu
from jax.sharding import PartitionSpec as P

ITERS = 3

teacher_temp = 0.07
student_temp = 0.1
epsilon = 1e-06
LOG2E = 1.4426950408889634
BF = jnp.bfloat16
F32 = jnp.float32
MIB = 1024 * 1024
BLK = 512
LANES = 128


def dot(a, b):
    return jnp.dot(a, b, preferred_element_type=F32)


def split(values):
    high = values.astype(BF).astype(F32)
    return high, (values - high).astype(BF).astype(F32)


def split_rows(row):
    high, low = split(row)
    at = lax.broadcasted_iota(jnp.int32, (16, row.shape[1]), 0)
    return jnp.where(at == 0, high, jnp.where(at == 1, low, 0.0)).astype(BF)


def unit_rows(raw):
    values = raw.astype(F32)
    length = jnp.sqrt(jnp.sum(values * values, axis=1, keepdims=True) + epsilon)
    return values / length, length


def over(count, size, body, carry):
    if count <= 4:
        for i in range(count):
            carry = body(pl.ds(i * size, size), carry)
        return carry

    def step(i, carry):
        return body(pl.ds(pl.multiple_of(i * size, size), size), carry)

    return lax.fori_loop(0, count, step, carry)


def chunks(span):
    for at in range(0, span.size, 64):
        start = span.start + at
        yield pl.ds(start if isinstance(start, int) else pl.multiple_of(start, 64), 64)


def block(i):
    return pl.ds(pl.multiple_of(i * BLK, BLK), BLK)


def each_step(low, high, body):
    for i in range(low, high):
        body(i)


def in_turn(left, right):
    done = 0
    for k, run in enumerate(left):
        run()
        while done * len(left) < (k + 1) * len(right):
            right[done]()
            done += 1


def two_steps(steps, first, second):
    runs, result = first(0)
    in_turn(runs, [])
    for i in range(1, steps):
        carry = result()
        runs, result = first(i)
        in_turn(runs, second(i - 1, carry))
    in_turn(second(steps - 1, result()), [])


def lane_groups(values):
    out = values[:, :LANES]
    for at in range(LANES, values.shape[1], LANES):
        out = out + values[:, at : at + LANES]
    return out


def sublane_groups(values):
    return jnp.sum(values.reshape(-1, 8, values.shape[1]), axis=0)


def joined(total, nb, at=0):
    return total[at : at + nb] + total[at + nb : at + 2 * nb]


def blocks_of(crops):
    height = next(h for h in (768, 512, 256, crops) if crops % h == 0)
    return crops // height, height


def row_sums(nb, rows, acc, at=0):
    spans = [slice(at + i * rows, at + (i + 1) * rows) for i in range(nb)]
    return [jnp.sum(acc[span, :].T, axis=0, keepdims=True) for span in spans]


def put_sums(sums, out, at=0):
    for i, row in enumerate(sums):
        high, low = split(row)
        out[at + i : at + i + 1, :] = high
        out[at + len(sums) + i : at + len(sums) + i + 1, :] = low


def deal(hops, head, read, count, outs, kept, chips=0):
    many = 1 + len(hops)
    me = lax.axis_index("proto")
    digit = (me // hops[0]) % many
    for hop, out in zip((0, *hops), (kept, *outs)):
        out[0 : head.shape[0], :] = head[...].astype(out.dtype)
        for m in range(count // many):
            turn = (me // 2 % chips == m % chips).astype(jnp.int32) if chips else 0
            rows = read(m * many + (digit ^ (hop // hops[0]) ^ turn)).astype(out.dtype)
            at = head.shape[0] + m * rows.shape[0]
            out[at : at + rows.shape[0], :] = rows


def added(refs):
    acc = refs[0][...].astype(F32)
    for ref in refs[1:]:
        acc = acc + ref[...].astype(F32)
    return acc


def halves_kernel(teacher_ref, student_ref, out, sems):
    half = out.shape[0] * 2 // 3
    me = lax.axis_index("proto")
    start = pl.multiple_of(me % 2 * half, half)
    quarter = pl.multiple_of(start + me // 2 % 2 * (half // 2), half // 2)
    first = pltpu.make_async_copy(
        teacher_ref.at[pl.ds(start, half), :], out.at[0:half, :], sems.at[0]
    )
    second = pltpu.make_async_copy(
        student_ref.at[pl.ds(quarter, half // 2), :], out.at[half:, :], sems.at[1]
    )
    first.start()
    second.start()
    first.wait()
    second.wait()


def units_kernel(after, also, *refs):
    blocks, outs = refs[-3::-1], refs[-2:]
    start = 0
    for out in outs:
        size = out.shape[0] // len(blocks)
        for i, ref in enumerate(blocks):
            rows = unit_rows(ref[start : start + size, :])[0]
            out[i * size : (i + 1) * size, :] = rows.astype(BF)
        start += size


def quarters_kernel(after, mine, moved, out):
    size = mine.shape[0]
    out[0:size, :] = mine[...]
    out[size:, :] = moved[...]


def place_kernel(size, mine, other, out):
    far = mine.shape[0]
    me = lax.axis_index("proto")
    core, side = me % 2, me // 2 % 2
    for ref, own in ((mine, core), (other, 1 - core)):
        for k, (half, quarter) in enumerate(((own, side), (1 - own, 1 - side))):
            for i in range(far // (2 * size)):
                at = pl.multiple_of(half * far + (2 * i + quarter) * size, size)
                start = k * (far // 2) + i * size
                out[pl.ds(at, size), :] = ref[start : start + size, :]


def weights_kernel(wt_ref, ws_ref, wt_out, ws_out, turned_out, raw, sems):
    steps = wt_out.shape[0]

    def copy(i, which):
        src = (wt_ref, ws_ref)[which]
        return pltpu.make_async_copy(src.at[:, block(i)], raw.at[which, i], sems.at[which, i])

    for which in range(2):
        for i in range(steps):
            copy(i, which).start()

    def unit(i, which):
        copy(i, which).wait()
        values = raw[which, i].astype(F32)
        length = jnp.sqrt(jnp.sum(values * values, axis=0, keepdims=True) + epsilon)
        return (values * ((LOG2E / (teacher_temp, student_temp)[which]) / length)).astype(BF)

    def teacher(i):
        wt_out[i] = unit(i, 0)

    def student(i):
        ws = unit(i, 1)
        ws_out[i] = ws
        turned_out[i] = ws.T

    each_step(0, steps, teacher)
    each_step(0, steps, student)


def add_across(rows, refs, i, ps, acc):
    own, rest = refs
    ps = ps.astype(BF)

    def add(ref, at, to):
        scaled = ref[i, at, :] * ps
        half = scaled[:, : BLK // 2] + scaled[:, BLK // 2 :]
        acc[to, :] += lane_groups(half.astype(F32))

    def many():
        def step(span, carry):
            for at in chunks(span):
                add(rest, at, pl.ds(at.start + rows, at.size))
            return carry

        over(*blocks_of(rest.shape[1]), step, 0)

    runs = [functools.partial(add, own, at, at) for at in chunks(pl.ds(0, rows))]
    if rest.shape[1] > 1024:
        return runs + [many]
    for at in chunks(pl.ds(0, rest.shape[1])):
        runs.append(functools.partial(add, rest, at, pl.ds(at.start + rows, at.size)))
    return runs


def own_first_kernel(own, wt_ref, e_ref, cols_ref, zt):
    zt[...] = unit_rows(own[...])[0].astype(BF)

    def body(i):
        e = jnp.exp2(dot(zt[...], wt_ref[i]))
        e_ref[i] = e.astype(BF)
        cols_ref[i] = sublane_groups(e)

    each_step(0, wt_ref.shape[0], body)


def exps_of(side, units, i, wt_ref, e_ref, cell):
    far = units.shape[0]
    height = 384 if far % 384 == 0 else 128
    logits = [None]

    def multiply(span):
        logits[0] = dot(units[span, :], wt_ref[i])

    def put(k, start):
        e = jnp.exp2(logits[0][k * 64 : (k + 1) * 64, :])
        e_ref[i, pl.ds(pl.multiple_of(side * far + start, 64), 64), :] = e.astype(BF)
        cell[0] = cell[0] + sublane_groups(e)

    def step(span, total):
        cell[0] = total
        multiply(span)
        for k, at in enumerate(chunks(span)):
            put(k, at.start)
        return cell[0]

    def many():
        cell[0] = over(far // height, height, step, cell[0])

    if far > height:
        return [many]
    runs = [functools.partial(multiply, pl.ds(0, far))]
    return runs + [functools.partial(put, k, k * 64) for k in range(far // 64)]


def mine_first_kernel(mine, wt_ref, own_cols, e_ref, cols_ref):
    side = lax.axis_index("proto") % 2

    def body(i):
        cell = [own_cols[i]]
        in_turn(exps_of(side, mine, i, wt_ref, e_ref, cell), [])
        cols_ref[i] = cell[0]

    each_step(0, wt_ref.shape[0], body)


def first_kernel(nb, begun, *refs):
    mine, other, wt_ref, own_ref, cols_ref, e_ref, out_ref, acc = refs[begun:]
    rows = own_ref.shape[1]
    side = lax.axis_index("proto") % 2
    acc[...] = jnp.zeros_like(acc)

    def exps(i):
        cell = [cols_ref[i]]
        runs = exps_of(1 - side, other, i, wt_ref, e_ref, cell)
        if not begun:
            runs = runs + exps_of(side, mine, i, wt_ref, e_ref, cell)
        return runs, lambda: 1.0 / jnp.sum(cell[0], axis=0, keepdims=True)

    refs = (own_ref, e_ref)
    two_steps(wt_ref.shape[0], exps, lambda i, ps: add_across(rows, refs, i, ps, acc))
    for i, row in enumerate(row_sums(nb, rows, acc)):
        out_ref[i : i + 1, :] = row


def start_sweep(nb, sums, cs, turned, acc):
    width = sums.shape[1]
    for i in range(nb):
        scale = 1.0 / sums[i : i + 1]
        span = slice(i * width, (i + 1) * width)
        if i < 2:
            turned[span, :] = jnp.broadcast_to(scale, (LANES, width)).T.astype(BF)
        else:
            cs[:, span] = split_rows(scale)
    acc[...] = jnp.zeros_like(acc)


def proto_scale(refs, i, cs, turned):
    own, rest = refs
    rows = own.shape[1]
    cell, down = [jnp.zeros((8, BLK), F32)], [None]

    def multiply():
        down[0] = dot(cs[:, 2 * rows :], rest[i, rows:, :])

    def add(ref, start, at):
        scale = turned[start + at.start : start + at.start + 64, :]
        scaled = ref[i, at, :] * jnp.concatenate([scale] * (BLK // LANES), axis=1)
        cell[0] = cell[0] + sublane_groups((scaled[:32] + scaled[32:]).astype(F32))

    runs = [multiply]
    for ref, start in ((own, 0), (rest, rows)):
        runs += [functools.partial(add, ref, start, at) for at in chunks(pl.ds(0, rows))]

    def result():
        total = jnp.sum(cell[0], axis=0, keepdims=True) + jnp.sum(down[0], axis=0, keepdims=True)
        return 1.0 / total

    return runs, result


def sweep_kernel(nb, after, x_ref, own_ref, e_ref, out_ref, cs, turned, acc):
    rows = own_ref.shape[1]
    both = (own_ref, e_ref)
    start_sweep(nb, x_ref[...], cs, turned, acc)
    two_steps(
        e_ref.shape[0],
        lambda i: proto_scale(both, i, cs, turned),
        lambda i, ps: add_across(rows, both, i, ps, acc),
    )
    for i, row in enumerate(row_sums(nb, rows, acc)):
        out_ref[i : i + 1, :] = row


def last_sweep_kernel(nb, k, n, hops, chips, x_ref, own_ref, e_ref, ws_rows, student, own_tot, *refs):
    tots, ps_ref, kept, outs = refs[:k], refs[k], refs[k + 1], refs[k + 2 : -5]
    cs, turned, acc, head, grad = refs[-5:]
    rows = own_ref.shape[1]
    both = (own_ref, e_ref)
    start_sweep(nb, x_ref[...], cs, turned, acc)
    grad[...] = jnp.zeros_like(grad)

    def across(i, ps):
        def add_grad():
            ps_ref[i] = ps
            grad[...] += dot(own_ref[i] * ps.astype(BF), ws_rows[i])

        return [add_grad] + add_across(rows, both, i, ps, acc)

    two_steps(e_ref.shape[0], lambda i: proto_scale(both, i, cs, turned), across)
    head[...] = jnp.zeros_like(head)
    put_sums(row_sums(nb, rows, acc), head)
    tot = tots[0][...]
    for more in tots[1:]:
        tot = tot + more[...]
    put_sums([own_tot[...]] + [tot[i : i + 1] for i in range(nb - 1)], head, 2 * nb)
    part = rows // n

    def read(r):
        at = pl.ds(pl.multiple_of(r * part, part), part)
        fill = [jnp.zeros((16 - part, grad.shape[1]), F32)] if part < 16 else []
        return jnp.concatenate([grad[at, :], *fill, student[at, :], *fill], axis=0)

    deal(hops, head, read, n, outs, kept, chips)


def deal_kernel(nb, count, hops, *refs):
    k = len(refs) - 3 - len(hops)
    arrived, kept, outs, (head, sums) = refs[:k], refs[k], refs[k + 1 : -2], refs[-2:]
    total = added(arrived)
    head[...] = jnp.zeros_like(head)
    for at in (0, 2 * nb):
        both = joined(total, nb, at)
        put_sums([both[i : i + 1] for i in range(nb)], head, at)
    sums[...] = total[head.shape[0] :]
    size = sums.shape[0] // count

    def read(r):
        return sums[pl.ds(pl.multiple_of(r * size, size), size), :]

    deal(hops, head, read, count, outs, kept)


def own_student_kernel(own, ws_ref, turned_ref, zs_ref, tot_ref, grad, s_ref, acc):
    zs_ref[...] = unit_rows(own[...])[0].astype(BF)
    acc[...] = jnp.zeros_like(acc)
    grad[...] = jnp.zeros_like(grad)
    kept = s_ref.shape[0] > 1

    def body(i):
        s = jnp.exp2(dot(zs_ref[...], ws_ref[i]))
        acc[...] += lane_groups(s)
        s_ref[i if kept else 0] = s.astype(BF)
        grad[...] += dot(s.astype(BF), turned_ref[i])

    each_step(0, ws_ref.shape[0], body)
    tot_ref[...] = row_sums(1, own.shape[0], acc)[0]


def student_kernel(first, count, after, zs_ref, ws_ref, tot_ref, s_ref, acc):
    acc[...] = jnp.zeros_like(acc)
    kept = s_ref.shape[0] > 1
    rows = tot_ref.shape[1]

    def body(i):
        j = i if kept else 0

        def exps(span, carry):
            logits = dot(zs_ref[span, :], ws_ref[i + first])
            for k, at in enumerate(chunks(span)):
                s = jnp.exp2(logits[k * 64 : (k + 1) * 64, :])
                acc[at, :] += lane_groups(s)
                s_ref[j, at, :] = s.astype(BF)
            return carry

        over(zs_ref.shape[0] // rows, rows, exps, 0)

    each_step(0, count, body)
    for i, row in enumerate(row_sums(tot_ref.shape[0], rows, acc)):
        tot_ref[i : i + 1, :] = row


def scaled_features(zs_refs, sums, out):
    here, width = out.shape[0], zs_refs[0].shape[1]
    at = lax.broadcasted_iota(jnp.int32, (here, width), 1)
    row = lax.broadcasted_iota(jnp.int32, (here, width), 0)
    pick = jnp.where(at == row + lax.axis_index("batch") * here, 1.0, 0.0).astype(BF)
    rows = zs_refs[0].shape[0]
    i = 0
    for ref in zs_refs:
        for start in range(0, ref.shape[0], rows):
            turned = lax.dot_general(
                pick,
                ref[start : start + rows, :],
                (((1,), (1,)), ((), ())),
                preferred_element_type=F32,
            )
            out[:, i * rows : (i + 1) * rows] = (turned * (1.0 / sums[i : i + 1])).astype(BF)
            i += 1


def feature_kernel(nb, k, factor, *refs):
    arrived, (feats_ref, own_zs, zs_ref, share_ref, lhs, ratio) = refs[:k], refs[k:]
    part, width = share_ref.shape
    rows = feats_ref.shape[0]
    padded = max(part, 16)
    total = added(arrived)
    sums, tots = joined(total, nb), joined(total, nb, 2 * nb)
    teacher, student = total[-2 * padded :][:part], total[-padded:][:part]
    at = lax.broadcasted_iota(jnp.int32, (part, rows), 1)
    row = lax.broadcasted_iota(jnp.int32, (part, rows), 0)
    pick = at == row + (lax.axis_index("proto") ^ 1) * part
    crop_scale = 1.0 / jnp.sum(jnp.where(pick, sums[0:1], 0.0), axis=1, keepdims=True)
    prob_scale = 1.0 / jnp.sum(jnp.where(pick, tots[0:1], 0.0), axis=1, keepdims=True)
    raw = dot(jnp.where(pick, 1.0, 0.0).astype(BF), feats_ref[...])
    unit, length = unit_rows(raw)
    grad = factor * (student * prob_scale - teacher * crop_scale)
    along = jnp.sum(unit * grad, axis=1, keepdims=True)
    share_ref[...] = ((grad - unit * along) / length).astype(share_ref.dtype)

    scaled_features((own_zs, zs_ref), sums, lhs)
    for i in range(nb):
        span = slice(i * rows, (i + 1) * rows)
        scale = jnp.broadcast_to(sums[i : i + 1] / tots[i : i + 1], (LANES, rows)).T
        ratio[span, :] = scale.astype(BF)


def weight_kernel(first, count, factor, aliased, starts, *refs):
    own_e, e_ref, ps_ref, own_zs, zs_ref, lhs, ratio = refs[1 + aliased : 8 + aliased]
    sources, (out_ref, token, diff, put, sems) = refs[8 + aliased : -5], refs[-5:]
    token[...] = jnp.zeros_like(token)
    rows = own_e.shape[1]

    def copy(i):
        return pltpu.make_async_copy(put.at[i], out_ref.at[:, block(i + first)], sems.at[i])

    def body(i, own_s, s_ref):
        ps = ps_ref[i].astype(BF)

        def down(zs, s, e, start):
            def step(span, acc):
                to = pl.ds(span.start + start, span.size)
                if not starts:
                    diff[to, :] = jnp.exp2(dot(zs[span, :], s[...])).astype(BF)
                for at in chunks(span):
                    to = pl.ds(at.start + start, at.size)
                    scale = jnp.concatenate([ratio[to, :]] * (BLK // LANES), axis=1)
                    left = (s[at, :] if starts else diff[to, :]) * scale
                    diff[to, :] = left - e[i, at, :] * ps
                to = pl.ds(span.start + start, span.size)
                return acc + dot(lhs[:, to], diff[to, :])

            return step

        acc = over(1, rows, down(own_zs, own_s, own_e, 0), jnp.zeros((lhs.shape[0], BLK), F32))
        acc = over(zs_ref.shape[0] // rows, rows, down(zs_ref, s_ref, e_ref, rows), acc)
        put[i - first] = (factor * acc).astype(BF)
        copy(i - first).start()

    def run(low, high, pick):
        if low < high:
            each_step(low, high, lambda i: body(i, *pick(i)))

    if starts:
        own_s, *kept = sources
        for low, high, ref in zip(starts, starts[1:], kept):
            run(
                max(low, first),
                min(high, first + count),
                lambda i, low=low, ref=ref: (own_s.at[i], ref.at[i - low]),
            )
    else:
        run(first, first + count, lambda i: (sources[0].at[i], sources[0].at[i]))
    for i in range(count):
        copy(i).wait()


def join_kernel(hops, after, share, *refs):
    moved, out_ref = refs[:-1], refs[-1]
    rows = share.shape[0]
    me = lax.axis_index("proto") ^ 1
    for hop, ref in zip((0, *hops[::-1]), (share, *moved)):
        place = ((me ^ hop) // hops[0]) % (1 + len(hops))
        out_ref[pl.ds(pl.multiple_of(place * rows, rows), rows), :] = ref[...].astype(out_ref.dtype)


def last_join_kernel(hops, after, share, *refs):
    moved, out_ref, sems = refs[:-2], refs[-2], refs[-1]
    rows = share.shape[0]
    me = lax.axis_index("proto") ^ 1
    copies = []
    for k, (hop, ref) in enumerate(zip((0, *hops[::-1]), (share, *moved))):
        place = ((me ^ hop) // hops[0]) % (1 + len(hops))
        to = out_ref.at[pl.ds(pl.multiple_of(place * rows, rows), rows), :]
        copies.append(pltpu.make_async_copy(ref, to, sems.at[k]))
    for copy in copies:
        copy.start()
    for copy in copies:
        copy.wait()


def permute(value, axis, s):
    n = lax.axis_size(axis)
    return lax.ppermute(value, axis, [(i, i ^ s) for i in range(n)])


def stages(n):
    bits = n.bit_length() - 1
    pairs = [[1 << b, 2 << b, 3 << b] if b + 1 < bits else [1 << b] for b in range(1, bits, 2)]
    return [[1]] + pairs


def permutes(value, axis, hops):
    return [permute(value, axis, hop) for hop in reversed(hops)][::-1]


def crossed(hop):
    return hop | 1


def shards(teacher_feats, student_feats, teacher_weight, student_weight):
    rows, width = teacher_feats.shape
    protos = teacher_weight.shape[1]
    nb, n = lax.axis_size("batch"), lax.axis_size("proto")
    crops, protos_all = rows * nb, protos * n
    here, part = width // nb, rows // n
    padded = max(part, 16)
    large = -(-4 * nb // 16) * 16
    keep = crops * protos <= 8 * MIB
    big = crops * protos
    wide = width * protos
    steps = protos // BLK

    limit = (16 if keep else 56) * MIB

    vmem = pl.BlockSpec(memory_space=pltpu.VMEM)
    hbm = pl.BlockSpec(memory_space=pltpu.HBM)
    anywhere = pl.BlockSpec(memory_space=pl.ANY)

    def shape(*dims, dtype=F32):
        return jax.ShapeDtypeStruct(dims, dtype)

    def call(kernel, out_shape, scratch, flops, moved, exps, *args, far=(), after=(), aliases={}):
        far = [pltpu.with_memory_space_constraint(a, pltpu.HBM) for a in far]
        return pl.pallas_call(
            kernel,
            out_shape=out_shape,
            in_specs=[hbm] * len(far)
            + [anywhere] * len(after)
            + [vmem] * len(args),
            out_specs=[vmem] * len(out_shape),
            scratch_shapes=scratch,
            input_output_aliases=aliases,
            compiler_params=pltpu.CompilerParams(vmem_limit_bytes=limit),
            cost_estimate=pl.CostEstimate(
                flops=int(flops), bytes_accessed=int(moved), transcendentals=int(exps)
            ),
        )(*far, *after, *args)

    def weight_call(kernel, out_shape, scratch, flops, moved, done, after, *args):
        return pl.pallas_call(
            kernel,
            out_shape=[out_shape, shape(8, LANES)],
            in_specs=[hbm] * len(done) + [anywhere] + [vmem] * len(args),
            out_specs=[hbm, vmem],
            scratch_shapes=scratch,
            input_output_aliases={0: 0} if done else {},
            compiler_params=pltpu.CompilerParams(vmem_limit_bytes=limit),
            cost_estimate=pl.CostEstimate(
                flops=int(flops), bytes_accessed=int(moved), transcendentals=0
            ),
        )(*done, after, *args)

    rest, half = crops - rows, rows // 2
    turned_crops = pltpu.VMEM((16, crops), BF)
    lane_sums = pltpu.VMEM((crops, LANES), F32)
    rounds = stages(n)
    sizes = [steps * 3 // 8, steps - steps * 3 // 8]
    weight_sizes = [steps // 8, steps - steps // 8]

    (mine,) = call(
        halves_kernel,
        [shape(half * 3 // 2, width, dtype=BF)],
        [pltpu.SemaphoreType.DMA((2,))],
        0,
        4 * rows * width,
        0,
        far=(teacher_feats, student_feats),
    )
    blocks = permutes(mine, "batch", range(1, nb))

    unit_wt, unit_ws, turned_ws = call(
        weights_kernel,
        [shape(steps, width, BLK, dtype=BF)] * 2 + [shape(steps, BLK, width, dtype=BF)],
        [pltpu.VMEM((2, steps, width, BLK), BF), pltpu.SemaphoreType.DMA((2, steps))],
        16 * wide,
        10 * wide,
        0,
        far=(teacher_weight, student_weight),
    )
    own_e, own_cols = call(
        own_first_kernel,
        [shape(steps, rows, BLK, dtype=BF), shape(steps, 8, BLK)],
        [pltpu.VMEM((rows, width), BF)],
        2 * rows * protos * width,
        2 * rows * protos,
        rows * protos,
        teacher_feats,
        unit_wt,
    )
    own_zs, own_tot, grad, own_s = call(
        own_student_kernel,
        [
            shape(rows, width, dtype=BF),
            shape(1, rows),
            shape(rows, width),
            shape(steps if keep else 1, rows, BLK, dtype=BF),
        ],
        [pltpu.VMEM((rows, LANES), F32)],
        4 * rows * protos * width,
        2 * rows * protos,
        rows * protos,
        student_feats,
        unit_ws,
        turned_ws,
    )

    mine, quarters = call(
        units_kernel,
        [shape(rest // 2, width, dtype=BF), shape(rest // 4, width, dtype=BF)],
        [],
        8 * crops * width,
        2 * crops * width,
        0,
        *reversed(blocks),
        after=(own_cols, own_tot),
    )
    other = permute(mine, "proto", 1)
    moved = permute(quarters, "proto", crossed(2))

    begun, cols = (), own_cols
    if keep:
        *begun, cols = call(
            mine_first_kernel,
            [shape(steps, rest, BLK, dtype=BF), shape(steps, 8, BLK)],
            [],
            rest * protos * width,
            rest * protos,
            rest * protos // 2,
            mine,
            unit_wt,
            own_cols,
        )
    e, x = call(
        functools.partial(first_kernel, nb, len(begun)),
        [shape(steps, rest, BLK, dtype=BF), shape(nb, width)],
        [lane_sums],
        2 * big * width,
        2 * big,
        big,
        *begun,
        mine,
        other,
        unit_wt,
        own_e,
        cols,
        aliases={0: 0} if begun else {},
    )
    (student_mine,) = call(
        quarters_kernel,
        [shape(rest // 2, width, dtype=BF)],
        [],
        0,
        2 * rest * width,
        0,
        quarters,
        moved,
        after=(x,),
    )
    (zs,) = call(
        functools.partial(place_kernel, half // 2),
        [shape(rest, width, dtype=BF)],
        [],
        0,
        4 * rest * width,
        0,
        student_mine,
        permute(student_mine, "proto", 1),
    )

    tots, kept = [], []

    def student_piece(after):
        k = len(kept)
        tot, piece = call(
            functools.partial(student_kernel, sum(sizes[:k]), sizes[k]),
            [shape(nb - 1, rows), shape(sizes[k] if keep else 1, rest, BLK, dtype=BF)],
            [pltpu.VMEM((rest, LANES), F32)],
            2 * rest * width * BLK * sizes[k],
            2 * rest * BLK * sizes[k],
            rest * BLK * sizes[k],
            zs,
            unit_ws,
            after=(after,),
        )
        tots.append(tot)
        kept.append(piece)

    def summed(x, pieces):
        for k, hops in enumerate(rounds):
            moved = permutes(x, "proto", [crossed(hop) for hop in hops])
            if k in pieces:
                student_piece(x)
            for value in reversed(moved):
                x = x + value
        return x

    x = summed(x, ())
    (x,) = call(
        functools.partial(sweep_kernel, nb),
        [shape(nb, width)],
        [turned_crops, pltpu.VMEM((2 * rows, LANES), BF), lane_sums],
        4 * big,
        2 * big,
        0,
        x,
        own_e,
        e,
        after=(zs,),
    )
    x = summed(x, (0, 1))

    def dealt(count, many):
        height = large + count // many * 2 * padded
        return [shape(height, width)] + [shape(height, width, dtype=BF)] * (many - 1)

    scale, *x = call(
        functools.partial(last_sweep_kernel, nb, len(tots), n, rounds[0], 1 + len(rounds[1])),
        [shape(steps, 1, BLK)] + dealt(n, 1 + len(rounds[0])),
        [
            turned_crops,
            pltpu.VMEM((2 * rows, LANES), BF),
            lane_sums,
            pltpu.VMEM((large, width), F32),
            pltpu.VMEM((rows, width), F32),
        ],
        4 * big,
        2 * big,
        0,
        x,
        own_e,
        e,
        turned_ws,
        grad,
        own_tot,
        *tots,
    )
    count = n
    for k, hops in enumerate(rounds):
        pairs = [crossed(hop) if k == 1 else hop for hop in hops]
        moved = [permute(x[1 + i], "proto", pairs[i]) for i in reversed(range(len(pairs)))]
        x = [x[0]] + moved
        count //= 1 + len(hops)
        if k + 1 < len(rounds):
            x = call(
                functools.partial(deal_kernel, nb, count, rounds[k + 1]),
                dealt(count, 1 + len(rounds[k + 1])),
                [pltpu.VMEM((large, width), F32), pltpu.VMEM((count * 2 * padded, width), F32)],
                4 * count * padded * width,
                8 * count * padded * width,
                0,
                *x,
            )

    factor = protos_all * math.sqrt(width / protos_all) * (student_temp / LOG2E)
    share, lhs, ratio = call(
        functools.partial(feature_kernel, nb, len(x), factor),
        [
            shape(part, width, dtype=BF if part % 16 == 0 else F32),
            shape(here, crops, dtype=BF),
            shape(crops, LANES, dtype=BF),
        ],
        [],
        0,
        8 * rows * width,
        0,
        *x,
        student_feats,
        own_zs,
        zs,
    )

    done = ()
    for k, hops in enumerate(rounds):
        moved = permutes(share, "proto", [crossed(hop) for hop in hops])
        if k < len(weight_sizes):
            first, size = sum(weight_sizes[:k]), weight_sizes[k]
            *done, token = weight_call(
                functools.partial(
                    weight_kernel,
                    first,
                    size,
                    protos_all * math.sqrt(width / crops),
                    len(done),
                    [sum(sizes[:i]) for i in range(len(sizes) + 1)] if keep else [],
                ),
                shape(here, protos, dtype=BF),
                [
                    pltpu.VMEM((crops, BLK), BF),
                    pltpu.VMEM((size, here, BLK), BF),
                    pltpu.SemaphoreType.DMA((size,)),
                ],
                2 * big * here * size // steps,
                4 * big * size // steps,
                done,
                share,
                own_e,
                e,
                scale,
                own_zs,
                zs,
                lhs,
                ratio,
                *((own_s, *kept) if keep else (unit_ws,)),
            )
        if k + 1 == len(rounds) and share.dtype == BF:
            (share,) = pl.pallas_call(
                functools.partial(last_join_kernel, hops),
                out_shape=[shape(rows, width, dtype=BF)],
                in_specs=[anywhere] + [vmem] * (1 + len(moved)),
                out_specs=[hbm],
                scratch_shapes=[pltpu.SemaphoreType.DMA((1 + len(moved),))],
                compiler_params=pltpu.CompilerParams(vmem_limit_bytes=limit),
            )(token, share, *reversed(moved))
            break
        (share,) = call(
            functools.partial(join_kernel, hops),
            [shape((1 + len(hops)) * share.shape[0], width, dtype=BF if k + 1 == len(rounds) else share.dtype)],
            [],
            0,
            8 * share.shape[0] * width,
            0,
            share,
            *reversed(moved),
            after=(token,),
        )
    return (done[0], share)


def solution(mesh):
    return jax.shard_map(
        shards,
        mesh=mesh,
        in_specs=(P("batch", None), P("batch", None), P(None, "proto"), P(None, "proto")),
        out_specs=(P("batch", "proto"), P("batch", None)),
        check_vma=False,
    )
```
